32 devices in a mesh: groups: 2 (over x), slab: 16 (over z, y, core).
Axes of the slice: x: 2, y: 2, z: 4, core: 2. Of those that a mesh axis runs over, the one named last changes fastest.
Arguments:
- latent: bfloat16 [64, 32, 2048], P(None, ('groups', 'slab')), parts along dimension 1, may hold values from -6 to 6
- conv1_weight: bfloat16 [27, 64, 64], replicated, may hold values from -0.15625 to 0.15625
- conv2_weight: bfloat16 [27, 64, 64], replicated, may hold values from -0.15625 to 0.15625
- head: bfloat16 [64], replicated, may hold values from -2 to 2
- p_prev: float32 [32, 16, 64, 128], P(('groups', 'slab')), parts along dimension 0, may hold values from -6 to 6
- p_cur: float32 [32, 16, 64, 128], P(('groups', 'slab')), parts along dimension 0, may hold values from -6 to 6
- adjoint: bfloat16 [4, 32, 16, 64, 128], P(None, ('groups', 'slab')), parts along dimension 1, may hold values from -6 to 6
- wavelet: float32 [16, 4], P('groups'), parts along dimension 0, may hold values from -12 to 12
- sources: int32 [16, 3], P('groups'), parts along dimension 0, may hold values from 0 to 127, as said below
- receivers: int32 [16, 3, 128], P('groups'), parts along dimension 0, may hold values from 0 to 127, as said below
Outputs:
- pressure_final: float32 [32, 16, 64, 128], P(('groups', 'slab')), parts along dimension 0
- traces: float32 [16, 4, 128], P('groups'), parts along dimension 0
- gradient: float32 [32, 2048], P(('groups', 'slab')), parts along dimension 0
The draws below stay inside these ranges and needn't reach their ends.
There are 2 independent parts, one for each index of `groups`. The reference program is written for one: setup_inputs(seed, part) draws one part's arguments, and reference() takes and returns one part's arrays. A program takes and returns all parts, laid end to end along the dimension named above; an argument that names none is the same for every part. Nothing has to cross between parts.
Inputs may be any that keep to these rules, and one draw needn't show every extreme that they name: sources[s] is the source cell (depth, row, column) of shot s on the fine grid: depth below 32, row below 64, column below 128. receivers[s, :, k] is the cell (depth, row, column) of receiver k of shot s on the fine grid: depth below 32, row below 64, column below 128.
All inputs are finite; a program needn't handle non-finite values.
Results may differ from the reference program's by a relative error of at most 0.006.
Values may be sent and summed in bfloat16 or wider, within the bound.
A program may use at most 64 MiB of HBM per device.

```python
import jax
import jax.numpy as jnp
from jax import lax

CH = 64
CY = 32
CX = 64
SHOTS = 8
STEPS = 4
NREC = 128
SLABS = 2
NZC = 16
FZ = 32
FPS = 16
FY = 64
FX = 128
SLOTS = 16


def draw_sources(key, part):
    key_depth, key_row, key_col, key_pick = jax.random.split(jax.random.fold_in(key, 11), 4)
    depths = jax.random.randint(key_depth, (SHOTS,), 0, FZ)
    rows_drawn = jax.random.randint(key_row, (SHOTS,), 0, FY)
    cols_drawn = jax.random.randint(key_col, (SHOTS,), 0, FX)
    chosen = jax.random.randint(key_pick, (), 0, SHOTS)
    marked = jnp.arange(SHOTS) == chosen
    depths = jnp.where(marked, FZ - 1, depths)
    rows_drawn = jnp.where(marked, FY - 1, rows_drawn)
    cols_drawn = jnp.where(marked, FX - 1, cols_drawn)
    return jnp.stack([depths, rows_drawn, cols_drawn], axis=1).astype(jnp.int32)


def draw_receivers(key, part):
    key_depth, key_row, key_col, key_pick = jax.random.split(jax.random.fold_in(key, 23), 4)
    depths = jax.random.randint(key_depth, (SHOTS, NREC), 0, FZ)
    rows_drawn = jax.random.randint(key_row, (SHOTS, NREC), 0, FY)
    cols_drawn = jax.random.randint(key_col, (SHOTS, NREC), 0, FX)
    chosen = jax.random.randint(key_pick, (SHOTS, 1), 0, NREC)
    marked = jnp.arange(NREC)[None, :] == chosen
    depths = jnp.where(marked, FZ - 1, depths)
    rows_drawn = jnp.where(marked, FY - 1, rows_drawn)
    cols_drawn = jnp.where(marked, FX - 1, cols_drawn)
    return jnp.stack([depths, rows_drawn, cols_drawn], axis=1).astype(jnp.int32)


def block_levels(rng, shape, shards, smallest, top_value):
    def one(position, blocks):
        draws = jax.random.uniform(jax.random.fold_in(jax.random.fold_in(rng, 6), position), (blocks,), jnp.float32, smallest / len(shards), top_value / len(shards))
        return jnp.repeat(jnp.exp(draws), shape[position] // blocks).reshape((-1,) + (1,) * (len(shape) - position - 1))

    factor_of = one(*shards[0])
    for cut in shards[1:]:
        factor_of = factor_of * one(*cut)
    return factor_of


def scatter_about(rng, shape, width, bound, cuts=(), held_as=jnp.bfloat16):
    drawn = jax.random.normal(rng, shape, jnp.float32) * width
    if len(cuts) > 0:
        drawn = block_levels(rng, shape, cuts, -0.22, 0.18) * drawn
    return jnp.clip(drawn, min=-bound, max=bound).astype(held_as)


def setup_inputs(seed: int = 0, part: int = 0) -> dict:
    keys = jax.random.split(jax.random.key(seed), 11)
    own_keys = jax.random.split(jax.random.fold_in(keys[10], part), 11)
    latent = scatter_about(own_keys[0], (CH, NZC, CY * CX), 1.0, 6.0, ((1, 16),))
    conv1_weight = scatter_about(keys[1], (27, CH, CH), (27 * CH) ** -0.5, 0.15625)
    conv2_weight = scatter_about(keys[2], (27, CH, CH), (27 * CH) ** -0.5, 0.15625)
    head = scatter_about(keys[3], (CH,), (CH // 8) ** -0.5, 2.0)
    p_prev = scatter_about(own_keys[4], (SLOTS, FPS, FY, FX), 1.0, 6.0, ((0, 16),), jnp.float32)
    p_cur = scatter_about(own_keys[5], (SLOTS, FPS, FY, FX), 1.0, 6.0, ((0, 16),), jnp.float32)
    adjoint = scatter_about(own_keys[6], (STEPS, SLOTS, FPS, FY, FX), 1.0, 6.0, ((1, 16),))
    wavelet = scatter_about(own_keys[7], (SHOTS, STEPS), 3.0, 12.0, (), jnp.float32)
    sources = draw_sources(jax.random.fold_in(jax.random.fold_in(keys[10], part), 71), part)
    receivers = draw_receivers(jax.random.fold_in(jax.random.fold_in(keys[10], part), 71), part)
    return dict(latent=latent, conv1_weight=conv1_weight, conv2_weight=conv2_weight, head=head, p_prev=p_prev, p_cur=p_cur, adjoint=adjoint, wavelet=wavelet, sources=sources, receivers=receivers)


stencil_weights = (-205.0 / 72.0, 8.0 / 5.0, -1.0 / 5.0, 8.0 / 315.0, -1.0 / 560.0)
lowest_speed = 1.5
speed_range = 3.0
courant = 0.088
leak_slope = 0.2

def conv_layer(activation, weight):
    planes = activation.shape[1]
    cell_count = activation.shape[2]
    extended = jnp.pad(activation, ((0, 0), (1, 1), (CX + 1, CX + 1)))
    columns = jnp.arange(cell_count) % CX
    accumulated = jnp.zeros((weight.shape[1], planes, cell_count), jnp.float32)
    tap_index = 0
    for depth_off in range(3):
        for row_off in (-1, 0, 1):
            for col_off in (-1, 0, 1):
                begin_at = CX + 1 + row_off * CX + col_off
                piece = extended[:, depth_off:depth_off + planes, begin_at:begin_at + cell_count]
                column_valid = ((columns + col_off >= 0) & (columns + col_off < CX)).astype(jnp.float32)
                accumulated = accumulated + jnp.einsum('oi,izn->ozn', weight[tap_index], piece * column_valid, precision=lax.Precision.HIGHEST)
                tap_index += 1
    return accumulated

def double_axis(values, axis):
    length = values.shape[axis]
    lower_side = jnp.concatenate([lax.slice_in_dim(values, 0, 1, axis=axis), lax.slice_in_dim(values, 0, length - 1, axis=axis)], axis=axis)
    upper_side = jnp.concatenate([lax.slice_in_dim(values, 1, length, axis=axis), lax.slice_in_dim(values, length - 1, length, axis=axis)], axis=axis)
    even_part = 0.75 * values + 0.25 * lower_side
    odd_part = 0.75 * values + 0.25 * upper_side
    new_shape = list(values.shape)
    new_shape[axis] = 2 * length
    return jnp.stack([even_part, odd_part], axis=axis + 1).reshape(new_shape)

def upsample_whole(coarse):
    grid = coarse.reshape(coarse.shape[0], CY, CX)
    return double_axis(double_axis(double_axis(grid, 0), 1), 2)

def stencil(extended):
    depth_total = extended.shape[0] - 8
    row_total = extended.shape[1]
    col_total = extended.shape[2]
    padded = jnp.pad(extended, ((0, 0), (4, 4), (4, 4)))

    def window(depth_at, row_at, col_at):
        return padded[depth_at:depth_at + depth_total, row_at:row_at + row_total, col_at:col_at + col_total]
    accumulated = 3.0 * stencil_weights[0] * window(4, 4, 4)
    for reach in range(1, 5):
        near_sum = window(4 - reach, 4, 4) + window(4 + reach, 4, 4)
        near_sum = near_sum + window(4, 4 - reach, 4) + window(4, 4 + reach, 4)
        near_sum = near_sum + window(4, 4, 4 - reach) + window(4, 4, 4 + reach)
        accumulated = accumulated + stencil_weights[reach] * near_sum
    return accumulated

def propagate(prev_field, field, adjoint_shot, pulses, source, station, courant_sq):
    correlation = jnp.zeros(field.shape, jnp.float32)
    samples_list = []
    for step_index in range(STEPS):
        laplace_term = stencil(jnp.pad(field, ((4, 4), (0, 0), (0, 0))))
        correlation = correlation + adjoint_shot[step_index].astype(jnp.float32) * laplace_term
        advanced = 2.0 * field - prev_field + courant_sq * laplace_term
        advanced = advanced.at[source[0], source[1], source[2]].add(pulses[step_index])
        samples_list.append(advanced[station[0], station[1], station[2]])
        prev_field, field = (field, advanced)
    return (field, jnp.stack(samples_list), correlation)

def reference(latent, conv1_weight, conv2_weight, head, p_prev, p_cur, adjoint, wavelet, sources, receivers):
    hidden = jax.nn.leaky_relu(conv_layer(latent.astype(jnp.float32), conv1_weight.astype(jnp.float32)), leak_slope).astype(jnp.bfloat16)
    second = jax.nn.leaky_relu(conv_layer(hidden.astype(jnp.float32), conv2_weight.astype(jnp.float32)), leak_slope)
    logits = jnp.einsum('c,czn->zn', head.astype(jnp.float32), second, precision=lax.Precision.HIGHEST)
    speed = (lowest_speed + speed_range * jax.nn.sigmoid(logits)).astype(jnp.bfloat16)
    coarse_speed = speed.astype(jnp.float32)
    fine_speed = upsample_whole(coarse_speed)
    courant_sq = (courant * fine_speed) ** 2

    def to_shots(field):
        return field.reshape(SLABS, SHOTS, FPS, FY, FX).transpose(1, 0, 2, 3, 4).reshape(SHOTS, FZ, FY, FX)
    prev_shots = to_shots(p_prev)
    cur_shots = to_shots(p_cur)
    adjoint_shots = adjoint.reshape(STEPS, SLABS, SHOTS, FPS, FY, FX).transpose(2, 0, 1, 3, 4, 5).reshape(SHOTS, STEPS, FZ, FY, FX)

    def one_shot(carried, inputs):
        prev_field, field, adjoint_shot, pulses, source, station = inputs
        final_field, samples, correlation = propagate(prev_field, field, adjoint_shot, pulses, source, station, courant_sq)
        return (carried + correlation, (final_field, samples))
    start_sum = jnp.zeros((FZ, FY, FX), jnp.float32)
    summed, outputs = lax.scan(one_shot, start_sum, (prev_shots, cur_shots, adjoint_shots, wavelet, sources, receivers))
    final_fields, traces = outputs
    pressure_final = final_fields.reshape(SHOTS, SLABS, FPS, FY, FX).transpose(1, 0, 2, 3, 4).reshape(SLOTS, FPS, FY, FX)
    fine_gradient = 2.0 * courant * courant * fine_speed * summed
    unused, pullback = jax.vjp(upsample_whole, coarse_speed)
    gradient = pullback(fine_gradient)[0]
    return (pressure_final, traces, gradient)
```

```python
import functools

import jax
import jax.numpy as jnp
import numpy as np
from jax import lax
from jax.experimental import pallas as pl
from jax.experimental.pallas import tpu as pltpu
from jax.sharding import PartitionSpec as P

CY = 32
CX = 64
CELLS = CY * CX
CH = 64
SHOTS = 8
STEPS = 4
FPS = 16
FY = 64
FX = 128
VMEM_BYTES = 60 * 2**20
PARTS = 4

C = (-205.0 / 72.0, 8.0 / 5.0, -1.0 / 5.0, 8.0 / 315.0, -1.0 / 560.0)
COURANT = 0.088
LEAK = 0.2
F32 = jnp.float32
BF16 = jnp.bfloat16


def banded(n):
    t = np.zeros((n, n), np.float64)
    for k in range(5):
        for i in range(n):
            for j in {i - k, i + k}:
                if 0 <= j < n:
                    t[i, j] = C[k]
    hi = t.astype(jnp.bfloat16).astype(np.float64)
    return hi, t - hi


def doubling(n):
    u = np.zeros((2 * n, n))
    for k in range(n):
        u[2 * k, k] += 0.75
        u[2 * k, max(k - 1, 0)] += 0.25
        u[2 * k + 1, k] += 0.75
        u[2 * k + 1, min(k + 1, n - 1)] += 0.25
    return u


def constants():
    hi, lo = banded(FX)
    along_x = np.concatenate([hi, hi, lo], axis=0)
    hi, lo = banded(FY)
    four = np.eye(4)
    along_y = np.concatenate([np.kron(four, hi), np.kron(four, hi), np.kron(four, lo)], axis=1)
    depth = np.zeros((FPS, SHOTS + 2))
    for k in range(SHOTS):
        depth[2 * k, k + 1] = 0.75
        depth[2 * k, k] = 0.25
        depth[2 * k + 1, k + 1] = 0.75
        depth[2 * k + 1, k + 2] = 0.25
    rows = doubling(CY)
    up_zy = np.concatenate([np.kron(depth, rows[:, 0::2]), np.kron(depth, rows[:, 1::2])], axis=1)
    up_x = np.kron(np.eye(2), doubling(CX).T)
    out = (along_x, along_y, up_zy, up_zy.T, up_x, up_x.T)
    return [jnp.asarray(a.astype(jnp.bfloat16)) for a in out]


def dot(a, b, dims=((1,), (0,))):
    return lax.dot_general(a, b, (dims, ((), ())), preferred_element_type=F32)


def two(v):
    hi = v.astype(BF16)
    return hi, (v - hi.astype(F32)).astype(BF16)


def kernel(
    n,
    latent,
    w1_hbm,
    w2_hbm,
    head_hbm,
    wavelet_hbm,
    sources_hbm,
    receivers_hbm,
    along_x_hbm,
    along_y_hbm,
    up_x_hbm,
    up_xt_hbm,
    prev_hbm,
    cur_hbm,
    adj_hbm,
    up_zy_hbm,
    up_zyt_hbm,
    final_out,
    traces_out,
    gradient_out,
    head,
    w1,
    w2,
    wavelet,
    sources,
    receivers,
    along_x,
    along_y,
    up_x,
    up_xt,
    lap0,
    head_col,
    a1,
    a2,
    wp1,
    wp2,
    y,
    vel,
    vels,
    field,
    adj,
    up_zy,
    up_zyt,
    speed,
    corr,
    rim_out,
    rim_in,
    hot,
    rec,
    recs,
    gr,
    grs,
    total,
    local_sem,
    lat_s,
    lat_r,
    hid_s,
    hid_r,
    rim_s,
    rim_r,
    vel_s,
    vel_r,
    rec_s,
    rec_r,
    gr_s,
    gr_r,
):
    me = lax.axis_index("slab")
    shot = lax.rem(me, SHOTS)
    slab = me // SHOTS
    slabs = n // SHOTS
    has_low = slab > 0
    has_high = slab < slabs - 1

    inner = pl.ds(4, FPS)
    pairs = (
        (latent, a1.at[1]),
        (w1_hbm, w1),
        (cur_hbm, field.at[1, inner]),
        (w2_hbm, w2),
        (receivers_hbm, receivers),
        (along_y_hbm, along_y),
        (along_x_hbm, along_x),
        (adj_hbm, adj),
        (up_x_hbm, up_x),
        (up_zy_hbm, up_zy),
        (wavelet_hbm, wavelet),
        (sources_hbm, sources),
        (prev_hbm, field.at[0, inner]),
        (up_zyt_hbm, up_zyt),
        (up_xt_hbm, up_xt),
        (head_hbm, head),
    )
    loads = [
        pltpu.make_async_copy(src, dst, local_sem.at[i]) for i, (src, dst) in enumerate(pairs)
    ]

    def remote(src, dst, send, recv, target):
        return pltpu.make_async_remote_copy(
            src_ref=src,
            dst_ref=dst,
            send_sem=send,
            recv_sem=recv,
            device_id={"slab": target},
            device_id_type=pl.DeviceIdType.MESH,
        )

    def peer(j):
        return lax.rem(me + j, n)

    barrier = pltpu.get_barrier_semaphore()

    def greet(j, carry):
        pl.semaphore_signal(
            barrier, inc=1, device_id={"slab": peer(j)}, device_id_type=pl.DeviceIdType.MESH
        )
        return carry

    lax.fori_loop(1, n, greet, 0)
    for load in loads:
        load.start()

    for a in (a1, a2):

        @pl.when(me == 0)
        def _():
            a[0] = jnp.zeros((CH, CELLS), BF16)

        @pl.when(me == n - 1)
        def _():
            a[2] = jnp.zeros((CH, CELLS), BF16)

    pl.semaphore_wait(barrier, n - 1)

    width = CELLS // PARTS

    def lat_copy(side, part):
        cols = pl.ds(part * width, width)
        return remote(
            latent.at[:, cols],
            a1.at[2 * side, :, cols],
            lat_s.at[side, part],
            lat_r.at[side, part],
            peer(1 if side == 0 else n - 1),
        )

    height = CH // PARTS

    def hid_copy(side, part):
        rows = pl.ds(pl.multiple_of(part * height, height), height)
        return remote(
            a2.at[1, rows],
            a2.at[2 * side, rows],
            hid_s.at[side, part],
            hid_r.at[side, part],
            peer(1 if side == 0 else n - 1),
        )

    def rim_copy(side, step):
        return remote(
            rim_out.at[side, step],
            rim_in.at[side, step],
            rim_s.at[side, step],
            rim_r.at[side, step],
            peer(SHOTS if side == 0 else n - SHOTS),
        )

    sends = (me < n - 1, me > 0)
    gets = (me > 0, me < n - 1)
    rim_sends = (has_high, has_low)
    rim_gets = (has_low, has_high)

    for part in range(PARTS):
        for side in range(2):

            @pl.when(sends[side])
            def _():
                lat_copy(side, part).start()

    loads[1].wait()
    loads[3].wait()
    for w, packed in ((w1, wp1), (w2, wp2)):
        for tap in range(9):
            for dz in range(3):
                packed[tap * CH : (tap + 1) * CH, dz * CH : (dz + 1) * CH] = w[dz * 9 + tap]

    loads[2].wait()
    rim_out[0, 0] = field[1, FPS : FPS + 4].reshape(4 * FY, FX).astype(BF16)
    rim_out[1, 0] = field[1, 4:8].reshape(4 * FY, FX).astype(BF16)
    @pl.when(jnp.logical_not(has_low))
    def _():
        field[:, 0:4] = jnp.zeros((2, 4, FY, FX), F32)

    @pl.when(jnp.logical_not(has_high))
    def _():
        field[:, FPS + 4 :] = jnp.zeros((2, 4, FY, FX), F32)

    loads[4].wait()
    loads[15].wait()
    station = receivers[:, shot]
    station_row = (station[0:1] - slab * FPS) * FY + station[1:2]
    station_col = station[2:3]
    hot[...] = (
        (lax.broadcasted_iota(jnp.int32, (FPS * FY, FX), 0) == station_row)
        .astype(F32)
        .astype(BF16)
    )
    col_hot = (lax.broadcasted_iota(jnp.int32, (FX, FX), 0) == station_col).astype(F32)
    rec[...] = jnp.zeros((8, FX), F32)

    square = (CH, CH)
    diagonal = lax.broadcasted_iota(jnp.int32, square, 0) == lax.broadcasted_iota(
        jnp.int32, square, 1
    )
    spread = jnp.broadcast_to(head[...].astype(F32), square)
    head_col[...] = jnp.broadcast_to(
        jnp.sum(jnp.where(diagonal, spread, 0.0), axis=1, keepdims=True), (CH, 128)
    )

    cell = lax.broadcasted_iota(jnp.int32, (1, CELLS), 1)
    col = lax.rem(cell, CX)
    keep_left = (col > 0).astype(F32)
    keep_right = (col < CX - 1).astype(F32)
    keep_up = (cell >= CX).astype(F32)
    keep_down = (cell < CELLS - CX).astype(F32)

    def multiply(packed, a, part):
        cols = slice(part * width, (part + 1) * width)
        block = jnp.concatenate([a[0, :, cols], a[1, :, cols], a[2, :, cols]], axis=0)
        y[:, :, cols] = dot(packed[...], block).reshape(9, CH, width)

    def gathered(first):
        sums = []
        for dx in range(3):
            above = y[dx, pl.ds(first, 8)]
            middle = y[3 + dx, pl.ds(first, 8)]
            below = y[6 + dx, pl.ds(first, 8)]
            sums.append(
                middle
                + keep_up * pltpu.roll(above, CX, 1)
                + keep_down * pltpu.roll(below, CELLS - CX, 1)
            )
        v = (
            sums[1]
            + keep_left * pltpu.roll(sums[0], 1, 1)
            + keep_right * pltpu.roll(sums[2], CELLS - 1, 1)
        )
        return jnp.where(v > 0, v, LEAK * v)

    loads[0].wait()
    for part in range(PARTS):
        for side in range(2):

            @pl.when(gets[side])
            def _():
                lat_copy(side, part).wait_recv()

        multiply(wp1, a1, part)

    for side in range(2):

        @pl.when(rim_sends[side])
        def _():
            rim_copy(side, 0).start()

    def hidden_part(part, carry):
        first = pl.multiple_of(part * height, height)
        pieces = [gathered(pl.multiple_of(first + 8 * h, 8)) for h in range(height // 8)]
        a2[1, pl.ds(first, height)] = jnp.concatenate(pieces, axis=0).astype(BF16)
        for side in range(2):

            @pl.when(sends[side])
            def _():
                hid_copy(side, part).start()

        return carry

    lax.fori_loop(0, PARTS, hidden_part, 0)
    def in_plane(cur, chunks):
        centres = [field[cur, 4 + 4 * c : 8 + 4 * c].reshape(4 * FY, FX) for c in chunks]
        halves = [two(v) for v in centres]
        across = jnp.concatenate(
            [jnp.concatenate([hi, lo, hi], axis=0) for hi, lo in halves], axis=1
        )
        from_rows = dot(along_y[...], across)
        laps = []
        for i, c in enumerate(chunks):
            hi, lo = halves[i]
            lap = from_rows[:, FX * i : FX * (i + 1)]
            lap = lap + dot(jnp.concatenate([hi, lo, hi], axis=1), along_x[...])
            laps.append(lap + C[0] * centres[i])
        return laps

    def in_depth(cur, chunks, laps):
        whole = []
        for c, lap in zip(chunks, laps):
            at = 4 + 4 * c
            for k in range(1, 5):
                near = field[cur, at - k : at - k + 4] + field[cur, at + k : at + k + 4]
                lap = lap + C[k] * near.reshape(4 * FY, FX)
            whole.append(lap)
        return whole

    def laplace(cur, chunks):
        return in_depth(cur, chunks, in_plane(cur, chunks))

    def advance(t, cur, old, c, lap):
        at = 4 + 4 * c
        courant = COURANT * speed[4 * FY * c : 4 * FY * (c + 1)]
        pulse = jnp.where(linear == source_at - c * 4 * FY * FX, wavelet[t, shot], 0.0)
        v = field[cur, at : at + 4].reshape(4 * FY, FX)
        before = field[old, at : at + 4].reshape(4 * FY, FX)
        new = 2.0 * v - before + courant * courant * lap + pulse
        field[old, at : at + 4] = new.reshape(4, FY, FX)

    def weighted(t, c, lap):
        return adj[t, 4 * c : 4 * c + 4].reshape(4 * FY, FX).astype(F32) * lap

    def take_rims(t, cur):
        for side in range(2):

            @pl.when(rim_gets[side])
            def _():
                rim_copy(side, t).wait_recv()
                at = (FPS + 4) * side
                field[cur, at : at + 4] = rim_in[side, t].reshape(4, FY, FX).astype(F32)

    def give_rims(t, old):
        rim_out[0, t + 1] = field[old, FPS : FPS + 4].reshape(4 * FY, FX).astype(BF16)
        rim_out[1, t + 1] = field[old, 4:8].reshape(4 * FY, FX).astype(BF16)
        for side in range(2):

            @pl.when(rim_sends[side])
            def _():
                rim_copy(side, t + 1).start()

    def record(t, old):
        hi, lo = two(field[old, 4 : 4 + FPS].reshape(FPS * FY, FX))
        seen = dot(hi, hot[...], ((0,), (0,))) + dot(lo, hot[...], ((0,), (0,)))
        seen = jnp.sum(seen * col_hot, axis=0, keepdims=True)
        rec[...] += jnp.where(lax.broadcasted_iota(jnp.int32, (8, FX), 0) == t, seen, 0.0)

    for i in (5, 6, 7, 8, 9, 10, 11, 12):
        loads[i].wait()
    source_at = (
        (sources[0, shot] - slab * FPS) * (FY * FX) + sources[1, shot] * FX + sources[2, shot]
    )
    linear = lax.broadcasted_iota(jnp.int32, (4 * FY, FX), 0) * FX + lax.broadcasted_iota(
        jnp.int32, (4 * FY, FX), 1
    )

    take_rims(0, 1)
    for chunks in ((0, 3), (1, 2)):
        for c, lap in zip(chunks, laplace(1, chunks)):
            rows = slice(4 * FY * c, 4 * FY * (c + 1))
            lap0[rows] = lap
            corr[rows] = weighted(0, c, lap)
    for part in range(PARTS):
        for side in range(2):

            @pl.when(gets[side])
            def _():
                hid_copy(side, part).wait_recv()

    for part in range(PARTS):
        multiply(wp2, a2, part)

    def logit_part(part, acc):
        first = pl.multiple_of(part * 8, 8)
        return acc + head_col[pl.ds(first, 8), 0:1] * gathered(first)

    logits = jnp.sum(
        lax.fori_loop(0, CH // 8, logit_part, jnp.zeros((8, CELLS), F32)), axis=0, keepdims=True
    )
    wave_speed = 1.5 + 3.0 / (1.0 + jnp.exp(-logits))
    rows16 = jnp.concatenate(
        [wave_speed[:, FX * j : FX * (j + 1)] for j in range(CELLS // FX)], axis=0
    )
    vel[...] = rows16.astype(BF16)

    def vel_copy(j):
        return remote(vel, vels.at[j], vel_s.at[j], vel_r.at[j], peer(j))

    def rec_copy(j):
        return remote(rec, recs.at[j], rec_s.at[j], rec_r.at[j], peer(j))

    def over_peers(what):
        def one(j, carry):
            what(j)
            return carry

        lax.fori_loop(1, n, one, 0)

    over_peers(lambda j: vel_copy(j).start())
    vels[0] = vel[...]
    over_peers(lambda j: vel_copy(j).wait_recv())

    planes = []
    for i in range(SHOTS + 2):
        plane = jnp.clip(slab * SHOTS - 1 + i, 0, n - 1)
        planes.append(vels[lax.rem(me - plane + n, n)])
    wide = dot(jnp.concatenate(planes, axis=0), up_x[...])
    tall = jnp.concatenate([wide[:, :FX], wide[:, FX:]], axis=0)
    hi, lo = two(tall)
    speed[...] = dot(up_zy[...], hi) + dot(up_zy[...], lo)

    def step(t, carry):
        cur = lax.rem(t + 1, 2)
        old = lax.rem(t, 2)
        outer, middle = (0, 3), (1, 2)
        laps = in_plane(cur, outer)
        take_rims(t, cur)
        laps = in_depth(cur, outer, laps)
        for c, lap in zip(outer, laps):
            advance(t, cur, old, c, lap)
        pl.when(t < STEPS - 1)(lambda: give_rims(t, old))
        laps = laps + laplace(cur, middle)
        for c, lap in zip(middle, laps[2:]):
            advance(t, cur, old, c, lap)
        for c, lap in zip(outer + middle, laps):
            corr[4 * FY * c : 4 * FY * (c + 1)] += weighted(t, c, lap)
        record(t, old)
        return carry

    for chunks in ((0, 3), (1, 2)):
        for c in chunks:
            advance(0, 1, 0, c, lap0[4 * FY * c : 4 * FY * (c + 1)])
        if chunks[0] == 0:
            give_rims(0, 0)
    record(0, 0)
    lax.fori_loop(1, STEPS, step, 0)
    store = pltpu.make_async_copy(
        field.at[(STEPS + 1) % 2, inner], final_out, local_sem.at[len(pairs)]
    )
    store.start()
    over_peers(lambda j: rec_copy(j).start())

    fine = (2.0 * COURANT * COURANT) * speed[...] * corr[...]
    hi, lo = two(fine)
    loads[13].wait()
    loads[14].wait()
    tall = dot(up_zyt[...], hi) + dot(up_zyt[...], lo)
    half = tall.shape[0] // 2
    hi, lo = two(jnp.concatenate([tall[:half], tall[half:]], axis=1))
    narrow = dot(hi, up_xt[...]) + dot(lo, up_xt[...])
    gr[...] = narrow.reshape(SHOTS + 2, 16, FX)

    @pl.when(jnp.logical_not(has_low))
    def _():
        gr[1] += gr[0]

    @pl.when(jnp.logical_not(has_high))
    def _():
        gr[SHOTS] += gr[SHOTS + 1]

    def gr_copy(j):
        other = lax.rem(shot + j, SHOTS)
        return remote(
            gr.at[other + 1], grs.at[j], gr_s.at[j], gr_r.at[j], slab * SHOTS + other
        )

    def low_copy(slot):
        return remote(
            gr.at[0], grs.at[slot], gr_s.at[8], gr_r.at[slot], lax.rem(slab * SHOTS - 1 + n, n)
        )

    def high_copy(slot):
        return remote(
            gr.at[SHOTS + 1],
            grs.at[slot],
            gr_s.at[9],
            gr_r.at[slot],
            lax.rem((slab + 1) * SHOTS, n),
        )

    @pl.when(has_low)
    def _():
        low_copy(8 + shot).start()

    @pl.when(has_high)
    def _():
        high_copy(16 + shot).start()

    for j in range(1, SHOTS):
        gr_copy(j).start()


    recs[0] = rec[...]
    over_peers(lambda j: rec_copy(j).wait_recv())
    for s in range(SHOTS):

        def slab_term(k, acc):
            return acc + recs[lax.rem(me - (k * SHOTS + s) + n, n)]

        summed = lax.fori_loop(0, slabs, slab_term, jnp.zeros((8, FX), F32))
        traces_out[s] = summed[:STEPS]

    total[...] = gr[shot + 1]
    for j in range(1, SHOTS):
        gr_copy(j).wait_recv()
        total[...] += grs[j]

    @pl.when((shot == SHOTS - 1) & has_high)
    def _():
        for s in range(SHOTS):
            low_copy(8 + s).wait_recv()
            total[...] += grs[8 + s]

    @pl.when((shot == 0) & has_low)
    def _():
        for s in range(SHOTS):
            high_copy(16 + s).wait_recv()
            total[...] += grs[16 + s]

    gradient_out[...] = total[...]

    store.wait()
    for part in range(PARTS):
        for side in range(2):

            @pl.when(sends[side])
            def _():
                lat_copy(side, part).wait_send()
                hid_copy(side, part).wait_send()

    for t in range(STEPS):
        for side in range(2):

            @pl.when(rim_sends[side])
            def _():
                rim_copy(side, t).wait_send()

    over_peers(lambda j: vel_copy(j).wait_send())
    over_peers(lambda j: rec_copy(j).wait_send())
    for j in range(1, SHOTS):
        gr_copy(j).wait_send()

    @pl.when(has_low)
    def _():
        low_copy(8 + shot).wait_send()

    @pl.when(has_high)
    def _():
        high_copy(16 + shot).wait_send()


def hand_over(a, b, c, x, y, z, sem):
    copies = [
        pltpu.make_async_copy(src, dst, sem.at[i])
        for i, (src, dst) in enumerate(((a, x), (b, y), (c, z)))
    ]
    for copy in copies:
        copy.start()
    for copy in copies:
        copy.wait()


def body(
    n,
    latent,
    conv1_weight,
    conv2_weight,
    head,
    p_prev,
    p_cur,
    adjoint,
    wavelet,
    sources,
    receivers,
):
    along_x, along_y, up_zy, up_zyt, up_x, up_xt = constants()
    vmem = pl.BlockSpec(memory_space=pltpu.VMEM)
    hbm = pl.BlockSpec(memory_space=pl.ANY)
    dma = pltpu.SemaphoreType.DMA
    final, traces, gradient = pl.pallas_call(
        functools.partial(kernel, n),
        out_shape=(
            pltpu.VMEM((FPS, FY, FX), F32),
            pltpu.VMEM((SHOTS, STEPS, 128), F32),
            pltpu.VMEM((16, FX), F32),
        ),
        in_specs=[hbm] * 16,
        out_specs=(vmem, vmem, vmem),
        scratch_shapes=[
            pltpu.VMEM((1, CH), BF16),
            pltpu.VMEM(conv1_weight.shape, BF16),
            pltpu.VMEM(conv2_weight.shape, BF16),
            pltpu.SMEM((STEPS, SHOTS), F32),
            pltpu.SMEM((3, SHOTS), jnp.int32),
            pltpu.VMEM((3, SHOTS, 128), jnp.int32),
            pltpu.VMEM(along_x.shape, BF16),
            pltpu.VMEM(along_y.shape, BF16),
            pltpu.VMEM(up_x.shape, BF16),
            pltpu.VMEM(up_xt.shape, BF16),
            pltpu.VMEM((FPS * FY, FX), F32),
            pltpu.VMEM((CH, 128), F32),
            pltpu.VMEM((3, CH, CELLS), BF16),
            pltpu.VMEM((3, CH, CELLS), BF16),
            pltpu.VMEM((9 * CH, 3 * CH), BF16),
            pltpu.VMEM((9 * CH, 3 * CH), BF16),
            pltpu.VMEM((9, CH, CELLS), F32),
            pltpu.VMEM((16, FX), BF16),
            pltpu.VMEM((n, 16, FX), BF16),
            pltpu.VMEM((2, FPS + 8, FY, FX), F32),
            pltpu.VMEM((STEPS, FPS, FY, FX), BF16),
            pltpu.VMEM(up_zy.shape, BF16),
            pltpu.VMEM(up_zyt.shape, BF16),
            pltpu.VMEM((FPS * FY, FX), F32),
            pltpu.VMEM((FPS * FY, FX), F32),
            pltpu.VMEM((2, STEPS, 4 * FY, FX), BF16),
            pltpu.VMEM((2, STEPS, 4 * FY, FX), BF16),
            pltpu.VMEM((FPS * FY, FX), BF16),
            pltpu.VMEM((8, FX), F32),
            pltpu.VMEM((n, 8, FX), F32),
            pltpu.VMEM((SHOTS + 2, 16, FX), F32),
            pltpu.VMEM((3 * SHOTS, 16, FX), F32),
            pltpu.VMEM((16, FX), F32),
            dma((17,)),
            dma((2, PARTS)),
            dma((2, PARTS)),
            dma((2, PARTS)),
            dma((2, PARTS)),
            dma((2, STEPS)),
            dma((2, STEPS)),
            dma((n,)),
            dma((n,)),
            dma((n,)),
            dma((n,)),
            dma((10,)),
            dma((3 * SHOTS,)),
        ],
        compiler_params=pltpu.CompilerParams(
            collective_id=0, has_side_effects=True, vmem_limit_bytes=VMEM_BYTES
        ),
    )(
        latent.reshape(CH, CELLS),
        conv1_weight,
        conv2_weight,
        head.reshape(1, CH),
        wavelet.T,
        sources.T,
        receivers.transpose(1, 0, 2),
        along_x,
        along_y,
        up_x,
        up_xt,
        p_prev[0],
        p_cur[0],
        adjoint[:, 0],
        up_zy,
        up_zyt,
    )
    final, traces, gradient = pl.pallas_call(
        hand_over,
        out_shape=(
            jax.ShapeDtypeStruct((FPS, FY, FX), F32),
            jax.ShapeDtypeStruct((SHOTS, STEPS, 128), F32),
            jax.ShapeDtypeStruct((16, FX), F32),
        ),
        in_specs=[vmem] * 3,
        out_specs=[hbm] * 3,
        scratch_shapes=[dma((3,))],
    )(*[pltpu.with_memory_space_constraint(v, pltpu.VMEM) for v in (final, traces, gradient)])
    return final[None], traces, gradient.reshape(1, CELLS)


def solution(mesh):
    in_specs = (
        P(None, ("groups", "slab"), None),
        P(),
        P(),
        P(),
        P(("groups", "slab"), None, None, None),
        P(("groups", "slab"), None, None, None),
        P(None, ("groups", "slab"), None, None, None),
        P("groups", None),
        P("groups", None),
        P("groups", None, None),
    )
    out_specs = (
        P(("groups", "slab"), None, None, None),
        P("groups", None, None),
        P(("groups", "slab"), None),
    )
    return jax.shard_map(
        functools.partial(body, mesh.shape["slab"]),
        mesh=mesh,
        in_specs=in_specs,
        out_specs=out_specs,
        check_vma=False,
    )
```

```python
import functools

import jax
import jax.numpy as jnp
import numpy as np
from jax import lax
from jax.experimental import pallas as pl
from jax.experimental.pallas import tpu as pltpu
from jax.sharding import PartitionSpec as P

CY = 32
CX = 64
CELLS = CY * CX
CH = 64
SHOTS = 8
STEPS = 4
FPS = 16
FY = 64
FX = 128
VMEM_BYTES = 60 * 2**20
PAIRS = ((0, 3), (3, 5), (5, 7), (7, 8))
FIRST = ((1, 2, 3, 4), (5, 6, 7, 8), (9, 10, 11, 12), (13, 14, 15, 0))
PIECES = ((1, 5), (5, 9), (9, 13), (13, 16), (0, 1))
SECOND = ((2, 3), (4, 5, 6, 7), (8, 9, 10, 11), (12, 13, 14, 15, 0, 1))
COLS = CY // 2

C = (-205.0 / 72.0, 8.0 / 5.0, -1.0 / 5.0, 8.0 / 315.0, -1.0 / 560.0)
BLOCK = 4 * FY
WINDOW = 8 * BLOCK
GROUP = 7
SCALE = 5040.0
CENTRE = 3.0 * SCALE * C[0]
COURANT = 0.088
LEAK = 0.2
F32 = jnp.float32
BF16 = jnp.bfloat16


def near(i, j):
    k = abs(i - j)
    return SCALE * C[k] if 1 <= k <= 4 else 0.0


def banded(n):
    return np.array([[near(i, j) for j in range(n)] for i in range(n)])


def doubling(n):
    u = np.zeros((2 * n, n))
    for k in range(n):
        u[2 * k, k] += 0.75
        u[2 * k, max(k - 1, 0)] += 0.25
        u[2 * k + 1, k] += 0.75
        u[2 * k + 1, min(k + 1, n - 1)] += 0.25
    return u


def constants():
    along_x = np.concatenate([banded(FX)] * 2, axis=0)
    along_y = np.concatenate([np.kron(np.eye(4), banded(FY))] * 2, axis=1)
    depth = np.zeros((FPS, SHOTS + 2))
    for k in range(SHOTS):
        depth[2 * k, k + 1] = 0.75
        depth[2 * k, k] = 0.25
        depth[2 * k + 1, k + 1] = 0.75
        depth[2 * k + 1, k + 2] = 0.25
    rows = doubling(CY)
    seven = np.eye(GROUP)
    up_y = np.concatenate(
        [np.kron(seven, rows[:, : CY // 2]), np.kron(seven, rows[:, CY // 2 :])], axis=1
    )
    down_zy = np.concatenate([np.kron(depth, rows[:, 0::2]), np.kron(depth, rows[:, 1::2])], axis=1).T
    eye = np.eye(CX)
    fold = np.zeros((2, 4, 4))
    for i, o in ((0, 0), (1, 2), (2, 1), (3, 3)):
        fold[0, i, o] = 1
    for i, o in ((0, 1), (3, 2)):
        fold[1, i, o] = 1
    fold = np.concatenate([np.kron(fold[0], eye), np.kron(fold[1], eye)], axis=0)
    up_x = np.kron(np.eye(2), doubling(CX).T)
    down_zy = np.stack(np.split(down_zy, 2, axis=1))
    out = (along_x, along_y, up_y, down_zy, up_x, up_x.T, fold)
    return [jnp.asarray(a.astype(jnp.bfloat16)) for a in out]


def dot(a, b, dims=((1,), (0,))):
    return lax.dot_general(a, b, (dims, ((), ())), preferred_element_type=F32)


def two(v):
    hi = v.astype(BF16)
    return hi, (v - hi.astype(F32)).astype(BF16)


def kernel(
    n,
    latent,
    w1_hbm,
    w2_hbm,
    head_hbm,
    wavelet_hbm,
    sources_hbm,
    receivers_hbm,
    along_x_hbm,
    along_y_hbm,
    up_x_hbm,
    up_xt_hbm,
    prev_hbm,
    cur_hbm,
    adj_hbm,
    up_y_hbm,
    up_zyt_hbm,
    fold_hbm,
    final_out,
    traces_out,
    gradient_out,
    head,
    w1,
    w2,
    wavelet,
    sources,
    receivers,
    along_x,
    along_y,
    up_x,
    up_xt,
    lap1,
    head_col,
    raw,
    fold,
    a1,
    a2,
    wp1,
    wp2,
    logits,
    vel,
    vels,
    f0,
    f1,
    f2,
    f3,
    f4,
    b1,
    b3,
    adj,
    up_y,
    up_zyt,
    speed,
    corr,
    pace,
    edge0,
    halo0,
    hot,
    seen,
    rec,
    recs,
    gr,
    grs,
    total,
    local_sem,
    lat_s,
    lat_r,
    hid_s,
    hid_r,
    rim_s,
    rim_r,
    vel_s,
    vel_r,
    rec_s,
    rec_r,
    gr_s,
    gr_r,
):
    me = lax.axis_index("slab")
    shot = lax.rem(me, SHOTS)
    slab = me // SHOTS
    slabs = n // SHOTS
    has_low = slab > 0
    has_high = slab < slabs - 1

    sends = (me < n - 1, me > 0)
    gets = (me > 0, me < n - 1)
    inner = pl.ds(2 * BLOCK, 4 * BLOCK)
    pairs = (
        (latent, raw.at[1]),
        (w1_hbm, w1),
        (cur_hbm, f1.at[inner]),
        (w2_hbm, w2),
        (receivers_hbm, receivers),
        (along_y_hbm, along_y),
        (along_x_hbm, along_x),
        (adj_hbm, adj),
        (up_x_hbm, up_x),
        (up_y_hbm, up_y),
        (wavelet_hbm, wavelet),
        (sources_hbm, sources),
        (prev_hbm, f0.at[inner]),
        (up_zyt_hbm, up_zyt),
        (up_xt_hbm, up_xt),
        (head_hbm, head),
        (fold_hbm, fold),
    )
    loads = [
        pltpu.make_async_copy(src, dst, local_sem.at[i]) for i, (src, dst) in enumerate(pairs)
    ]

    def remote(src, dst, send, recv, target):
        return pltpu.make_async_remote_copy(
            src_ref=src,
            dst_ref=dst,
            send_sem=send,
            recv_sem=recv,
            device_id={"slab": target},
            device_id_type=pl.DeviceIdType.MESH,
        )

    def peer(j):
        return lax.rem(me + j, n)

    barrier = pltpu.get_barrier_semaphore()

    def over_peers(what):
        def one(j, carry):
            what(j)
            return carry

        if n <= 16:
            for j in range(1, n):
                what(j)
        else:
            lax.fori_loop(1, n, one, 0)

    def greet(j):
        pl.semaphore_signal(
            barrier, inc=1, device_id={"slab": peer(j)}, device_id_type=pl.DeviceIdType.MESH
        )

    over_peers(greet)
    for load in loads:
        load.start()

    for a in (raw, a2):
        for side in range(2):

            @pl.when(jnp.logical_not(gets[side]))
            def _():
                a[2 * side] = jnp.zeros(a.shape[1:], BF16)

    pl.semaphore_wait(barrier, n - 1)

    def lat_copy(side, part, half):
        first, end = PAIRS[part]
        cols = pl.ds((first + half * COLS // 2) * 128, (end - first) * 128)
        return remote(
            latent.at[:, cols],
            raw.at[2 * side, :, cols],
            lat_s.at[side],
            lat_r.at[side, part],
            peer(1 if side == 0 else n - 1),
        )

    def arrived(ref, sem):
        remote(ref, ref, sem, sem, me).wait_recv()

    def departed(ref, sem):
        remote(ref, ref, sem, sem, me).wait_send()

    def hid_copy(side, piece):
        first, end = PIECES[piece]
        cols = pl.ds((first + 1) * 128, (end - first) * 128)
        return remote(
            a2.at[1, :, cols],
            a2.at[2 * side, :, cols],
            hid_s.at[side],
            hid_r.at[side, min(piece, 3)],
            peer(1 if side == 0 else n - 1),
        )

    def rim_copy(side, what):
        block = (5, 2)[side]
        to = (1, 6)[side]
        out, back = (4, 0) if side == 0 else (3, 7)
        if what == 0:
            src, dst = b1.at[pl.ds(block * BLOCK, BLOCK)], b1.at[pl.ds(to * BLOCK, BLOCK)]
        elif what == 1:
            src, dst = b1.at[pl.ds(out * BLOCK, BLOCK)], b1.at[pl.ds(back * BLOCK, BLOCK)]
        elif what == 2:
            src, dst = edge0.at[side], halo0.at[side]
        else:
            first, back = (4, 0) if side == 0 else (2, 6)
            src = b3.at[pl.ds(first * BLOCK, 2 * BLOCK)]
            dst = b3.at[pl.ds(back * BLOCK, 2 * BLOCK)]
        return remote(
            src,
            dst,
            rim_s.at[side, what // 3],
            rim_r.at[side, what // 3],
            peer(SHOTS if side == 0 else n - SHOTS),
        )

    rim_sends = (has_high, has_low)
    rim_gets = (has_low, has_high)

    def rows(b):
        return pl.ds(pl.multiple_of(b * BLOCK, BLOCK), BLOCK)

    def own(b):
        return pl.ds(pl.multiple_of((b - 2) * BLOCK, BLOCK), BLOCK)

    for part in range(len(PAIRS)):
        for side in range(2):

            @pl.when(sends[side])
            def _():
                lat_copy(side, part, 0).start()
                lat_copy(side, part, 1).start()

    loads[1].wait()
    loads[3].wait()
    for w, packed in ((w1, wp1), (w2, wp2)):
        for dx in range(3):
            packed[dx * CH : (dx + 1) * CH] = jnp.concatenate(
                [w[dz * 9 + dy * 3 + dx] for dy in range(3) for dz in range(3)], axis=1
            )

    for side in range(2):
        ext = (1, 6)[side]

        @pl.when(jnp.logical_not(rim_gets[side]))
        def _():
            for f in (f1, f2, f3, f4):
                f[ext * BLOCK : (ext + 1) * BLOCK] = jnp.zeros((BLOCK, FX), F32)

    loads[2].wait()
    loads[12].wait()
    b1[inner] = f1[inner].astype(BF16)
    edge0[0] = f0[5 * BLOCK : 6 * BLOCK].astype(BF16)
    edge0[1] = f0[2 * BLOCK : 3 * BLOCK].astype(BF16)
    loads[4].wait()
    loads[15].wait()
    station = receivers[:, shot]
    same = lax.broadcasted_iota(jnp.int32, (128, 128), 0) == lax.broadcasted_iota(
        jnp.int32, (128, 128), 1
    )

    def upright(v):
        return jnp.sum(
            jnp.where(same, jnp.broadcast_to(v.astype(F32), (128, 128)), 0.0), axis=1, keepdims=True
        ).astype(jnp.int32)

    station_row = upright((station[0:1] - slab * FPS) * FY + station[1:2])
    station_col = upright(station[2:3])
    row = lax.broadcasted_iota(jnp.int32, (128, BLOCK), 1)
    for b in range(4):
        hot[b] = (row + b * BLOCK == station_row).astype(F32).astype(BF16)
    at_col = lax.broadcasted_iota(jnp.int32, (128, FX), 1) == station_col
    seen[...] = jnp.zeros(seen.shape, F32)
    rec[...] = jnp.zeros((8, FX), F32)

    square = (CH, CH)
    diagonal = lax.broadcasted_iota(jnp.int32, square, 0) == lax.broadcasted_iota(
        jnp.int32, square, 1
    )
    spread = jnp.broadcast_to(head[...].astype(F32), square)
    head_col[...] = jnp.broadcast_to(
        jnp.sum(jnp.where(diagonal, spread, 0.0), axis=1, keepdims=True), (CH, 128)
    )

    lane = lax.broadcasted_iota(jnp.int32, (1, 128), 1)
    keep_left = lax.rem(lane, CX) > 0
    keep_right = lax.rem(lane, CX) < CX - 1

    def column(a, c):
        return a[:, :, c * 128 : (c + 1) * 128].reshape(3 * CH, 128)

    def put(a, c, v):
        a[:, :, c * 128 : (c + 1) * 128] = v.astype(BF16).reshape(3, CH, 128)

    def close(a):
        ends = jnp.concatenate([column(a, COLS), column(a, 1)], axis=1)
        moved = dot(ends, fold[256:])
        put(a, 0, moved[:, :128])
        put(a, COLS + 1, moved[:, 128:])

    def convolved(packed, a, columns):
        block = jnp.concatenate(
            [
                jnp.concatenate([column(a, j + dy) for dy in range(3)], axis=0)
                for j in columns
            ],
            axis=1,
        )
        taps = dot(packed[...], block)
        out = []
        for i in range(len(columns)):
            left, middle, right = (
                taps[dx * CH : (dx + 1) * CH, i * 128 : (i + 1) * 128] for dx in range(3)
            )
            v = (
                middle
                + jnp.where(keep_left, pltpu.roll(left, 1, 1), 0.0)
                + jnp.where(keep_right, pltpu.roll(right, 127, 1), 0.0)
            )
            out.append(jnp.where(v > 0, v, LEAK * v))
        return out

    loads[0].wait()
    loads[16].wait()

    def send_hidden(pieces):
        for side in range(2):

            @pl.when(sends[side])
            def _():
                for piece in pieces:
                    hid_copy(side, piece).start()

    for part, (first, end) in enumerate(PAIRS):
        for side in range(2):

            @pl.when(gets[side])
            def _():
                arrived(
                    raw.at[2 * side, :, pl.ds(0, 2 * (end - first) * 128)], lat_r.at[side, part]
                )

        for i in range(first, end):
            pair = jnp.concatenate([column(raw, i), column(raw, i + COLS // 2)], axis=1)
            folded = dot(pair, fold[:256])
            put(a1, 2 * i + 1, folded[:, :128])
            put(a1, 2 * i + 2, folded[:, 128:])
        if end == COLS // 2:
            close(a1)
        for j, v in zip(FIRST[part], convolved(wp1, a1, FIRST[part])):
            a2[1, :, (j + 1) * 128 : (j + 2) * 128] = v.astype(BF16)
        send_hidden((part, part + 1) if end == COLS // 2 else (part,))

    for what in range(3):
        for side in range(2):

            @pl.when(rim_sends[side])
            def _():
                rim_copy(side, what).start()

    def beside(now, c, planes):
        return now[pl.ds(pl.multiple_of(c * BLOCK + planes * FY, FY), BLOCK)]

    def laplace(now, blocks):
        centres = [now[rows(c)] for c in blocks]
        halves = [two(v) for v in centres]
        down = dot(
            along_y[...],
            jnp.concatenate([jnp.concatenate(h, axis=0) for h in halves], axis=1),
        )
        across = dot(
            jnp.concatenate([jnp.concatenate(h, axis=1) for h in halves], axis=0), along_x[...]
        )
        laps = []
        for i, (c, v) in enumerate(zip(blocks, centres)):
            lap = CENTRE * v + down[:, FX * i : FX * (i + 1)]
            lap = lap + across[BLOCK * i : BLOCK * (i + 1)]
            for k in range(1, 5):
                lap = lap + (SCALE * C[k]) * (beside(now, c, -k) + beside(now, c, k))
            laps.append(lap)
        return laps

    def advance(t, b, lap, v, before):
        pulse = jnp.where(linear == source_at - (b - 2) * (BLOCK * FX), wavelet[t - 1, shot], 0.0)
        return 2.0 * v - before + pace[rows(b)] * lap + pulse

    def weighted(t, b, lap):
        return adj[t - 1, own(b)].astype(F32) * lap

    def observe(t, b, new):
        hi, lo = two(new)
        got = dot(hot[b - 2], jnp.concatenate([hi, lo], axis=1))
        seen[t - 1] += got[:, :FX] + got[:, FX:]

    def finish(t, c, lap, now, before, new_f):
        new = advance(t, c, lap, now[rows(c)], before[rows(c)])
        new_f[(own if t == STEPS else rows)(c)] = new
        return new

    def step(t, blocks, now, before, new_f):
        for c, lap in zip(blocks, laplace(now, blocks)):
            finish(t, c, lap, now, before, new_f)
            corr[own(c)] += weighted(t, c, lap)

    for i in (5, 6, 7, 8, 9, 10, 11):
        loads[i].wait()
    source_at = (
        (sources[0, shot] - slab * FPS) * (FY * FX) + sources[1, shot] * FX + sources[2, shot]
    )
    linear = lax.broadcasted_iota(jnp.int32, (BLOCK, FX), 0) * FX + lax.broadcasted_iota(
        jnp.int32, (BLOCK, FX), 1
    )

    def first_laplace(blocks):
        for c, lap in zip(blocks, laplace(f1, blocks)):
            lap1[rows(c)] = lap
            corr[own(c)] = weighted(1, c, lap)

    first_laplace((3, 4))

    def get_hidden(piece):
        for side in range(2):

            @pl.when(gets[side])
            def _():
                arrived(a2.at[2 * side, :, pl.ds(128, 4 * 128)], hid_r.at[side, piece])

    for part, columns in enumerate(SECOND):
        get_hidden(part)
        if part == len(SECOND) - 1:
            close(a2)
        for j, v in zip(columns, convolved(wp2, a2, columns)):
            v = v * head_col[...]
            logits[8 * j : 8 * j + 8] = jnp.sum(v.reshape(CH // 8, 8, 128), axis=0)
    total_logits = jnp.sum(logits[...].reshape(COLS, 8, 128), axis=1)
    wave_speed = 1.5 + 3.0 / (1.0 + jnp.exp(-total_logits))
    vel[...] = wave_speed.astype(BF16)

    def vel_copy(k, to_slab, slot, send, recv):
        return remote(vel, vels.at[slot], vel_s.at[send], vel_r.at[recv], to_slab * SHOTS + k)

    lends_low = (shot <= 2) & has_low
    lends_high = (shot >= SHOTS - 3) & has_high

    def vel_sends():
        for j in range(1, SHOTS):
            vel_copy(lax.rem(shot + j, SHOTS), slab, shot + 3, 0, 0).start()

        @pl.when(lends_low)
        def _():
            for k in range(SHOTS):
                vel_copy(k, slab - 1, lax.rem(shot, 3) + 11, 1, 2).start()

        @pl.when(lends_high)
        def _():
            for k in range(SHOTS):
                vel_copy(k, slab + 1, lax.rem(shot + 1, 3), 1, 1).start()

    def vel_gets():
        arrived(vels.at[pl.ds(0, SHOTS - 1)], vel_r.at[0])
        for side in range(2):

            @pl.when(rim_gets[side])
            def _():
                arrived(vels.at[pl.ds(0, 3)], vel_r.at[side + 1])

    def rec_copy(j):
        return remote(rec, recs.at[j], rec_s.at[0], rec_r.at[0], peer(j))

    vel_sends()
    vels[shot + 3] = vel[...]
    for side in range(2):
        edge, ext = ((2, 1), (5, 6))[side]

        @pl.when(rim_gets[side])
        def _():
            arrived(b1.at[pl.ds(0, 3 * BLOCK)], rim_r.at[side, 0])

    first_laplace((2, 5))
    for side in range(2):
        ext = (1, 6)[side]

        @pl.when(rim_gets[side])
        def _():
            at = slice((0, 6)[side] * BLOCK, (2, 8)[side] * BLOCK)
            f1[at] = b1[at].astype(F32)
            f0[rows(ext)] = halo0[side].astype(F32)

    first_laplace((2, 5))
    for side in range(2):
        ext = (1, 6)[side]

        @pl.when(rim_gets[side])
        def _():
            lap1[rows(ext)] = laplace(f1, (ext,))[0]

    vel_gets()
    planes = []
    for i in range(2 * GROUP):
        plane = jnp.clip(slab * SHOTS - 3 + i, 0, n - 1)
        planes.append(vels[plane - slab * SHOTS + 3])
    wide = dot(jnp.concatenate(planes, axis=0), up_x[...])
    tall = []
    for g in range(2):
        part = wide[16 * GROUP * g : 16 * GROUP * (g + 1)]
        hi, lo = two(jnp.concatenate([part[:, :FX], part[:, FX:]], axis=0))
        both = dot(up_y[...], jnp.concatenate([hi, lo], axis=1))
        both = both[:, :FX] + both[:, FX:]
        tall += [both[FY * i : FY * (i + 1)] for i in range(GROUP)]
    for z in range(-4, FPS + 4):
        i = z // 2 + 3
        fine = 0.75 * tall[i] + 0.25 * tall[i + 1 if z % 2 else i - 1]
        at = z * FY + 2 * BLOCK
        if 0 <= z < FPS:
            speed[z * FY : (z + 1) * FY] = fine
        courant = COURANT * fine
        pace[at : at + FY] = courant * courant * (1.0 / SCALE)

    n1, n2 = jnp.where(has_low, 2, 5), jnp.where(has_low, 3, 4)
    g1, g2 = 7 - n1, 7 - n2
    far_too = has_low & has_high

    def second(c):
        finish(1, c, lap1[rows(c)], f1, f0, f2)

    for side in range(2):

        @pl.when(rim_gets[side])
        def _():
            second((1, 6)[side])

    for b in (2, 3, 4, 5):
        second(b)
    step(2, (n1, n2), f2, f1, f3)
    for c in (n1, n2):
        b3[rows(c)] = f3[rows(c)].astype(BF16)

    @pl.when(has_low)
    def _():
        rim_copy(1, 3).start()

    @pl.when(has_high & jnp.logical_not(has_low))
    def _():
        rim_copy(0, 3).start()

    step(2, (g1, g2), f2, f1, f3)

    @pl.when(far_too)
    def _():
        b3[4 * BLOCK : 6 * BLOCK] = f3[4 * BLOCK : 6 * BLOCK].astype(BF16)
        rim_copy(0, 3).start()

    for b in (2, 3, 4, 5):
        observe(1, b, f2[rows(b)])
        observe(2, b, f3[rows(b)])

    @pl.when(far_too)
    def _():
        rim_copy(1, 3).wait_recv()
        f3[6 * BLOCK :] = b3[6 * BLOCK :].astype(F32)
        finish(3, 6, laplace(f3, (6,))[0], f3, f2, f4)

    step(3, (g1, g2), f3, f2, f4)
    step(3, (n2,), f3, f2, f4)
    step(4, (g1, g2), f4, f3, final_out)
    for b in (g1, g2):
        observe(4, b, final_out[own(b)])
    for b in (g1, g2, n2):
        observe(3, b, f4[rows(b)])

    def collected(first):
        parts = []
        for t in (first, first + 1):
            parts += two(jnp.where(at_col, seen[t - 1], 0.0))
        wide = (8, 4 * FX)
        pick = lax.broadcasted_iota(jnp.int32, wide, 0) == first - 1 + lax.broadcasted_iota(
            jnp.int32, wide, 1
        ) // (2 * FX)
        rec[...] += dot(
            pick.astype(F32).astype(BF16), jnp.concatenate(parts, axis=1), ((1,), (1,))
        )

    collected(1)
    loads[13].wait()
    loads[14].wait()

    def raised(pair):
        at = pl.ds(pl.multiple_of(pair * 2 * BLOCK, 2 * BLOCK), 2 * BLOCK)
        fine = (2.0 * COURANT * COURANT / SCALE) * speed[at] * corr[at]
        return dot(up_zyt[pair], fine.astype(BF16))

    near_pair = jnp.where(has_low, 0, 1)
    tall = raised(1 - near_pair)
    @pl.when(has_low)
    def _():
        rim_copy(0, 3).wait_recv()

    @pl.when(has_high & jnp.logical_not(has_low))
    def _():
        rim_copy(1, 3).wait_recv()

    halo = pl.ds(pl.multiple_of(jnp.where(has_low, 0, 6 * BLOCK), 2 * BLOCK), 2 * BLOCK)
    ext = jnp.where(has_low, 1, 6)
    f3[halo] = b3[halo].astype(F32)
    lap_ext, lap = laplace(f3, (ext, n1))
    finish(3, ext, lap_ext, f3, f2, f4)
    finish(3, n1, lap, f3, f2, f4)
    corr[own(n1)] += weighted(3, n1, lap)
    step(4, (n1, n2), f4, f3, final_out)
    observe(3, n1, f4[rows(n1)])
    for b in (n1, n2):
        observe(4, b, final_out[own(b)])
    collected(3)
    tall = tall + raised(near_pair)
    half = tall.shape[0] // 2
    hi, lo = two(jnp.concatenate([tall[:half], tall[half:]], axis=1))
    narrow = dot(hi, up_xt[...]) + dot(lo, up_xt[...])
    gr[...] = narrow.reshape(SHOTS + 2, 16, FX)
    over_peers(lambda j: rec_copy(j).start())


    @pl.when(jnp.logical_not(has_low))
    def _():
        gr[1] += gr[0]

    @pl.when(jnp.logical_not(has_high))
    def _():
        gr[SHOTS] += gr[SHOTS + 1]

    def gr_copy(j):
        other = lax.rem(shot + j, SHOTS)
        return remote(
            gr.at[other + 1], grs.at[j], gr_s.at[0], gr_r.at[0], slab * SHOTS + other
        )

    def low_copy(slot):
        return remote(
            gr.at[0], grs.at[slot], gr_s.at[1], gr_r.at[1], lax.rem(slab * SHOTS - 1 + n, n)
        )

    def high_copy(slot):
        return remote(
            gr.at[SHOTS + 1],
            grs.at[slot],
            gr_s.at[2],
            gr_r.at[2],
            lax.rem((slab + 1) * SHOTS, n),
        )

    @pl.when(has_low)
    def _():
        low_copy(8 + shot).start()

    @pl.when(has_high)
    def _():
        high_copy(16 + shot).start()

    for j in range(1, SHOTS):
        gr_copy(j).start()


    recs[0] = rec[...]
    arrived(recs.at[pl.ds(1, n - 1)], rec_r.at[0])
    for s in range(SHOTS):

        def slab_term(k, acc):
            return acc + recs[lax.rem(me - (k * SHOTS + s) + n, n)]

        summed = lax.fori_loop(0, slabs, slab_term, jnp.zeros((8, FX), F32))
        traces_out[s] = summed[:STEPS]

    arrived(grs.at[pl.ds(1, SHOTS - 1)], gr_r.at[0])
    summed = gr[shot + 1]
    for j in range(1, SHOTS):
        summed = summed + grs[j]
    total[...] = summed

    @pl.when((shot == SHOTS - 1) & has_high)
    def _():
        arrived(grs.at[pl.ds(8, SHOTS)], gr_r.at[1])
        total[...] += jnp.sum(grs[8:16], axis=0)

    @pl.when((shot == 0) & has_low)
    def _():
        arrived(grs.at[pl.ds(16, SHOTS)], gr_r.at[2])
        total[...] += jnp.sum(grs[16:24], axis=0)

    gradient_out[...] = total[...]

    for side in range(2):

        @pl.when(sends[side])
        def _():
            departed(raw.at[0], lat_s.at[side])
            departed(a2.at[1, :, pl.ds(128, CELLS)], hid_s.at[side])

        @pl.when(rim_sends[side])
        def _():
            departed(b1.at[pl.ds(0, 3 * BLOCK)], rim_s.at[side, 0])
            departed(b3.at[pl.ds(0, 2 * BLOCK)], rim_s.at[side, 1])

    departed(vels.at[pl.ds(0, SHOTS - 1)], vel_s.at[0])

    @pl.when(lends_low | lends_high)
    def _():
        departed(vels.at[pl.ds(0, SHOTS)], vel_s.at[1])

    departed(recs.at[pl.ds(1, n - 1)], rec_s.at[0])
    departed(grs.at[pl.ds(1, SHOTS - 1)], gr_s.at[0])

    @pl.when(has_low)
    def _():
        departed(grs.at[0], gr_s.at[1])

    @pl.when(has_high)
    def _():
        departed(grs.at[0], gr_s.at[2])


def hand_over(a, b, c, x, y, z, sem):
    copies = [
        pltpu.make_async_copy(src, dst, sem.at[i])
        for i, (src, dst) in enumerate(((a, x), (b, y), (c, z)))
    ]
    for copy in copies:
        copy.start()
    for copy in copies:
        copy.wait()


def body(
    n,
    latent,
    conv1_weight,
    conv2_weight,
    head,
    p_prev,
    p_cur,
    adjoint,
    wavelet,
    sources,
    receivers,
):
    along_x, along_y, up_y, up_zyt, up_x, up_xt, fold = constants()
    vmem = pl.BlockSpec(memory_space=pltpu.VMEM)
    hbm = pl.BlockSpec(memory_space=pl.ANY)
    dma = pltpu.SemaphoreType.DMA
    final, traces, gradient = pl.pallas_call(
        functools.partial(kernel, n),
        out_shape=(
            pltpu.VMEM((FPS * FY, FX), F32),
            pltpu.VMEM((SHOTS, STEPS, 128), F32),
            pltpu.VMEM((16, FX), F32),
        ),
        in_specs=[hbm] * 17,
        out_specs=(vmem, vmem, vmem),
        scratch_shapes=[
            pltpu.VMEM((1, CH), BF16),
            pltpu.VMEM(conv1_weight.shape, BF16),
            pltpu.VMEM(conv2_weight.shape, BF16),
            pltpu.SMEM((STEPS, SHOTS), F32),
            pltpu.SMEM((3, SHOTS), jnp.int32),
            pltpu.VMEM((3, SHOTS, 128), jnp.int32),
            pltpu.VMEM(along_x.shape, BF16),
            pltpu.VMEM(along_y.shape, BF16),
            pltpu.VMEM(up_x.shape, BF16),
            pltpu.VMEM(up_xt.shape, BF16),
            pltpu.VMEM((WINDOW, FX), F32),
            pltpu.VMEM((CH, 128), F32),
            pltpu.VMEM((3, CH, CELLS), BF16),
            pltpu.VMEM(fold.shape, BF16),
            pltpu.VMEM((3, CH, (COLS + 2) * 128), BF16),
            pltpu.VMEM((3, CH, (COLS + 2) * 128), BF16),
            pltpu.VMEM((3 * CH, 9 * CH), BF16),
            pltpu.VMEM((3 * CH, 9 * CH), BF16),
            pltpu.VMEM((COLS * 8, 128), F32),
            pltpu.VMEM((16, FX), BF16),
            pltpu.VMEM((2 * GROUP, 16, FX), BF16),
            *[pltpu.VMEM((WINDOW, FX), F32)] * 5,
            *[pltpu.VMEM((WINDOW, FX), BF16)] * 2,
            pltpu.VMEM((STEPS, FPS * FY, FX), BF16),
            pltpu.VMEM(up_y.shape, BF16),
            pltpu.VMEM(up_zyt.shape, BF16),
            pltpu.VMEM((FPS * FY, FX), F32),
            pltpu.VMEM((FPS * FY, FX), F32),
            pltpu.VMEM((WINDOW, FX), F32),
            pltpu.VMEM((2, BLOCK, FX), BF16),
            pltpu.VMEM((2, BLOCK, FX), BF16),
            pltpu.VMEM((4, 128, BLOCK), BF16),
            pltpu.VMEM((STEPS, 128, FX), F32),
            pltpu.VMEM((8, FX), F32),
            pltpu.VMEM((n, 8, FX), F32),
            pltpu.VMEM((SHOTS + 2, 16, FX), F32),
            pltpu.VMEM((3 * SHOTS, 16, FX), F32),
            pltpu.VMEM((16, FX), F32),
            dma((18,)),
            dma((2,)),
            dma((2, 4)),
            dma((2,)),
            dma((2, 4)),
            dma((2, 2)),
            dma((2, 2)),
            dma((2,)),
            dma((3,)),
            dma((1,)),
            dma((1,)),
            dma((3,)),
            dma((3,)),
        ],
        compiler_params=pltpu.CompilerParams(
            collective_id=0, has_side_effects=True, vmem_limit_bytes=VMEM_BYTES
        ),
    )(
        latent.reshape(CH, CELLS),
        conv1_weight,
        conv2_weight,
        head.reshape(1, CH),
        wavelet.T,
        sources.T,
        receivers.transpose(1, 0, 2),
        along_x,
        along_y,
        up_x,
        up_xt,
        p_prev.reshape(FPS * FY, FX),
        p_cur.reshape(FPS * FY, FX),
        adjoint.reshape(STEPS, FPS * FY, FX),
        up_y,
        up_zyt,
        fold,
    )
    final, traces, gradient = pl.pallas_call(
        hand_over,
        out_shape=(
            jax.ShapeDtypeStruct((FPS * FY, FX), F32),
            jax.ShapeDtypeStruct((SHOTS, STEPS, 128), F32),
            jax.ShapeDtypeStruct((16, FX), F32),
        ),
        in_specs=[vmem] * 3,
        out_specs=[hbm] * 3,
        scratch_shapes=[dma((3,))],
    )(*[pltpu.with_memory_space_constraint(v, pltpu.VMEM) for v in (final, traces, gradient)])
    return final.reshape(1, FPS, FY, FX), traces, gradient.reshape(1, CELLS)


def solution(mesh):
    in_specs = (
        P(None, ("groups", "slab"), None),
        P(),
        P(),
        P(),
        P(("groups", "slab"), None, None, None),
        P(("groups", "slab"), None, None, None),
        P(None, ("groups", "slab"), None, None, None),
        P("groups", None),
        P("groups", None),
        P("groups", None, None),
    )
    out_specs = (
        P(("groups", "slab"), None, None, None),
        P("groups", None, None),
        P(("groups", "slab"), None),
    )
    return jax.shard_map(
        functools.partial(body, mesh.shape["slab"]),
        mesh=mesh,
        in_specs=in_specs,
        out_specs=out_specs,
        check_vma=False,
    )
```

```python
import functools

import jax
import jax.numpy as jnp
import numpy as np
from jax import lax
from jax.experimental import pallas as pl
from jax.experimental.pallas import tpu as pltpu
from jax.sharding import PartitionSpec as P

CY = 32
CX = 64
CELLS = CY * CX
CH = 64
SHOTS = 8
STEPS = 4
FPS = 16
FY = 64
FX = 128
VMEM_BYTES = 60 * 2**20
RIMS_AT = (-1,3,4)
HALVES = 1
PAIRS = ((0, 3), (3, 5), (5, 7), (7, 8))
FIRST = ((1, 2, 3, 4), (5, 6, 7, 8), (9, 10, 11, 12), (13, 14, 15, 0))
PIECES = ((1, 5), (5, 9), (9, 13), (13, 16), (0, 1))
SECOND = ((2, 3), (4, 5, 6, 7), (8, 9, 10, 11), (12, 13, 14, 15, 0, 1))
COLS = CY // 2

C = (-205.0 / 72.0, 8.0 / 5.0, -1.0 / 5.0, 8.0 / 315.0, -1.0 / 560.0)
BLOCK = 4 * FY
WINDOW = 8 * BLOCK
GROUP = 7
SCALE = 5040.0
CENTRE = 3.0 * SCALE * C[0]
COURANT = 0.088
LEAK = 0.2
F32 = jnp.float32
BF16 = jnp.bfloat16


def near(i, j):
    k = abs(i - j)
    return SCALE * C[k] if 1 <= k <= 4 else 0.0


def banded(n):
    return np.array([[near(i, j) for j in range(n)] for i in range(n)])


def doubling(n):
    u = np.zeros((2 * n, n))
    for k in range(n):
        u[2 * k, k] += 0.75
        u[2 * k, max(k - 1, 0)] += 0.25
        u[2 * k + 1, k] += 0.75
        u[2 * k + 1, min(k + 1, n - 1)] += 0.25
    return u


def constants():
    along_x = np.concatenate([banded(FX)] * 2, axis=0)
    along_y = np.concatenate([np.kron(np.eye(4), banded(FY))] * 2, axis=1)
    depth = np.zeros((FPS, SHOTS + 2))
    for k in range(SHOTS):
        depth[2 * k, k + 1] = 0.75
        depth[2 * k, k] = 0.25
        depth[2 * k + 1, k + 1] = 0.75
        depth[2 * k + 1, k + 2] = 0.25
    rows = doubling(CY)
    seven = np.eye(GROUP)
    up_y = np.concatenate(
        [np.kron(seven, rows[:, : CY // 2]), np.kron(seven, rows[:, CY // 2 :])], axis=1
    )
    down_zy = np.concatenate([np.kron(depth, rows[:, 0::2]), np.kron(depth, rows[:, 1::2])], axis=1).T
    eye = np.eye(CX)
    fold = np.zeros((2, 4, 4))
    for i, o in ((0, 0), (1, 2), (2, 1), (3, 3)):
        fold[0, i, o] = 1
    for i, o in ((0, 1), (3, 2)):
        fold[1, i, o] = 1
    fold = np.concatenate([np.kron(fold[0], eye), np.kron(fold[1], eye)], axis=0)
    up_x = np.kron(np.eye(2), doubling(CX).T)
    down_zy = np.stack(np.split(down_zy, 2, axis=1))
    out = (along_x, along_y, up_y, down_zy, up_x, up_x.T, fold)
    return [jnp.asarray(a.astype(jnp.bfloat16)) for a in out]


def dot(a, b, dims=((1,), (0,))):
    return lax.dot_general(a, b, (dims, ((), ())), preferred_element_type=F32)


def two(v):
    hi = v.astype(BF16)
    return hi, (v - hi.astype(F32)).astype(BF16)


def kernel(
    n,
    latent,
    w1_hbm,
    w2_hbm,
    head_hbm,
    wavelet_hbm,
    sources_hbm,
    receivers_hbm,
    along_x_hbm,
    along_y_hbm,
    up_x_hbm,
    up_xt_hbm,
    prev_hbm,
    cur_hbm,
    adj_hbm,
    up_y_hbm,
    up_zyt_hbm,
    fold_hbm,
    final_out,
    traces_out,
    gradient_out,
    head,
    w1,
    w2,
    wavelet,
    sources,
    receivers,
    along_x,
    along_y,
    up_x,
    up_xt,
    lap1,
    head_col,
    raw,
    fold,
    a1,
    a2,
    wp1,
    wp2,
    logits,
    vel,
    vels,
    f0,
    f1,
    f2,
    f3,
    f4,
    b1,
    b3,
    adj,
    up_y,
    up_zyt,
    speed,
    corr,
    pace,
    edge0,
    halo0,
    hot,
    seen,
    rec,
    recs,
    gr,
    grs,
    total,
    local_sem,
    lat_s,
    lat_r,
    hid_s,
    hid_r,
    rim_s,
    rim_r,
    vel_s,
    vel_r,
    rec_s,
    rec_r,
    gr_s,
    gr_r,
):
    me = lax.axis_index("slab")
    shot = lax.rem(me, SHOTS)
    slab = me // SHOTS
    slabs = n // SHOTS
    has_low = slab > 0
    has_high = slab < slabs - 1

    sends = (me < n - 1, me > 0)
    gets = (me > 0, me < n - 1)
    inner = pl.ds(2 * BLOCK, 4 * BLOCK)
    pairs = (
        (latent, raw.at[1]),
        (w1_hbm, w1),
        (cur_hbm, f1.at[inner]),
        (w2_hbm, w2),
        (receivers_hbm, receivers),
        (along_y_hbm, along_y),
        (along_x_hbm, along_x),
        (adj_hbm, adj),
        (up_x_hbm, up_x),
        (up_y_hbm, up_y),
        (wavelet_hbm, wavelet),
        (sources_hbm, sources),
        (prev_hbm, f0.at[inner]),
        (up_zyt_hbm, up_zyt),
        (up_xt_hbm, up_xt),
        (head_hbm, head),
        (fold_hbm, fold),
    )
    loads = [
        pltpu.make_async_copy(src, dst, local_sem.at[i]) for i, (src, dst) in enumerate(pairs)
    ]

    def remote(src, dst, send, recv, target):
        return pltpu.make_async_remote_copy(
            src_ref=src,
            dst_ref=dst,
            send_sem=send,
            recv_sem=recv,
            device_id={"slab": target},
            device_id_type=pl.DeviceIdType.MESH,
        )

    def peer(j):
        return lax.rem(me + j, n)

    barrier = pltpu.get_barrier_semaphore()

    def over_peers(what):
        def one(j, carry):
            what(j)
            return carry

        if n <= 16:
            for j in range(1, n):
                what(j)
        else:
            lax.fori_loop(1, n, one, 0)

    def greet(j):
        pl.semaphore_signal(
            barrier, inc=1, device_id={"slab": peer(j)}, device_id_type=pl.DeviceIdType.MESH
        )

    over_peers(greet)
    for load in loads:
        load.start()

    for a in (raw, a2):
        for side in range(2):

            @pl.when(jnp.logical_not(gets[side]))
            def _():
                a[2 * side] = jnp.zeros(a.shape[1:], BF16)

    pl.semaphore_wait(barrier, n - 1)

    def lat_copy(side, part, half):
        first, end = PAIRS[part]
        cols = pl.ds((first + half * COLS // 2) * 128, (end - first) * 128)
        return remote(
            latent.at[:, cols],
            raw.at[2 * side, :, cols],
            lat_s.at[side],
            lat_r.at[side, part],
            peer(1 if side == 0 else n - 1),
        )

    def arrived(ref, sem):
        remote(ref, ref, sem, sem, me).wait_recv()

    def departed(ref, sem):
        remote(ref, ref, sem, sem, me).wait_send()

    def hid_copy(side, piece):
        first, end = PIECES[piece]
        cols = pl.ds((first + 1) * 128, (end - first) * 128)
        return remote(
            a2.at[1, :, cols],
            a2.at[2 * side, :, cols],
            hid_s.at[side],
            hid_r.at[side, min(piece, 3)],
            peer(1 if side == 0 else n - 1),
        )

    def rim_copy(side, what):
        block = (5, 2)[side]
        to = (1, 6)[side]
        out, back = (4, 0) if side == 0 else (3, 7)
        if what == 0:
            src, dst = b1.at[pl.ds(block * BLOCK, BLOCK)], b1.at[pl.ds(to * BLOCK, BLOCK)]
        elif what == 1:
            src, dst = b1.at[pl.ds(out * BLOCK, BLOCK)], b1.at[pl.ds(back * BLOCK, BLOCK)]
        elif what == 2:
            src, dst = edge0.at[side], halo0.at[side]
        else:
            first, back = (4, 0) if side == 0 else (2, 6)
            src = b3.at[pl.ds(first * BLOCK, 2 * BLOCK)]
            dst = b3.at[pl.ds(back * BLOCK, 2 * BLOCK)]
        return remote(
            src,
            dst,
            rim_s.at[side, what // 3],
            rim_r.at[side, (what + 1) // 2],
            peer(SHOTS if side == 0 else n - SHOTS),
        )

    rim_sends = (has_high, has_low)
    rim_gets = (has_low, has_high)

    def rows(b):
        return pl.ds(pl.multiple_of(b * BLOCK, BLOCK), BLOCK)

    def own(b):
        return pl.ds(pl.multiple_of((b - 2) * BLOCK, BLOCK), BLOCK)

    for part in range(len(PAIRS)):
        for side in range(2):

            @pl.when(sends[side])
            def _():
                lat_copy(side, part, 0).start()
                lat_copy(side, part, 1).start()

    loads[1].wait()
    loads[3].wait()
    for w, packed in ((w1, wp1), (w2, wp2)):
        for dx in range(3):
            packed[dx * CH : (dx + 1) * CH] = jnp.concatenate(
                [w[dz * 9 + dy * 3 + dx] for dy in range(3) for dz in range(3)], axis=1
            )

    for side in range(2):
        ext = (1, 6)[side]

        @pl.when(jnp.logical_not(rim_gets[side]))
        def _():
            for f in (f1, f2, f3, f4):
                f[ext * BLOCK : (ext + 1) * BLOCK] = jnp.zeros((BLOCK, FX), F32)

    loads[2].wait()
    loads[12].wait()
    b1[inner] = f1[inner].astype(BF16)
    edge0[0] = f0[5 * BLOCK : 6 * BLOCK].astype(BF16)
    edge0[1] = f0[2 * BLOCK : 3 * BLOCK].astype(BF16)
    def give_rims(at):
        for what in range(3):
            for side in range(2):
                if RIMS_AT[what] == at:

                    @pl.when(rim_sends[side])
                    def _():
                        rim_copy(side, what).start()

    give_rims(-1)
    loads[4].wait()
    loads[15].wait()
    station = receivers[:, shot]
    same = lax.broadcasted_iota(jnp.int32, (128, 128), 0) == lax.broadcasted_iota(
        jnp.int32, (128, 128), 1
    )

    def upright(v):
        return jnp.sum(
            jnp.where(same, jnp.broadcast_to(v.astype(F32), (128, 128)), 0.0), axis=1, keepdims=True
        ).astype(jnp.int32)

    station_row = upright((station[0:1] - slab * FPS) * FY + station[1:2])
    station_col = upright(station[2:3])
    row = lax.broadcasted_iota(jnp.int32, (128, BLOCK), 1)
    for b in range(4):
        hot[b] = (row + b * BLOCK == station_row).astype(F32).astype(BF16)
    at_col = lax.broadcasted_iota(jnp.int32, (128, FX), 1) == station_col
    seen[...] = jnp.zeros(seen.shape, F32)
    rec[...] = jnp.zeros((STEPS, FX), F32)

    square = (CH, CH)
    diagonal = lax.broadcasted_iota(jnp.int32, square, 0) == lax.broadcasted_iota(
        jnp.int32, square, 1
    )
    spread = jnp.broadcast_to(head[...].astype(F32), square)
    head_col[...] = jnp.broadcast_to(
        jnp.sum(jnp.where(diagonal, spread, 0.0), axis=1, keepdims=True), (CH, 128)
    )

    lane = lax.broadcasted_iota(jnp.int32, (1, 128), 1)
    keep_left = lax.rem(lane, CX) > 0
    keep_right = lax.rem(lane, CX) < CX - 1

    def column(a, c):
        return a[:, :, c * 128 : (c + 1) * 128].reshape(3 * CH, 128)

    def put(a, c, v):
        a[:, :, c * 128 : (c + 1) * 128] = v.astype(BF16).reshape(3, CH, 128)

    def close(a):
        ends = jnp.concatenate([column(a, COLS), column(a, 1)], axis=1)
        moved = dot(ends, fold[256:])
        put(a, 0, moved[:, :128])
        put(a, COLS + 1, moved[:, 128:])

    def convolved(packed, a, columns):
        block = jnp.concatenate(
            [
                jnp.concatenate([column(a, j + dy) for dy in range(3)], axis=0)
                for j in columns
            ],
            axis=1,
        )
        taps = dot(packed[...], block)
        out = []
        for i in range(len(columns)):
            left, middle, right = (
                taps[dx * CH : (dx + 1) * CH, i * 128 : (i + 1) * 128] for dx in range(3)
            )
            v = (
                middle
                + jnp.where(keep_left, pltpu.roll(left, 1, 1), 0.0)
                + jnp.where(keep_right, pltpu.roll(right, 127, 1), 0.0)
            )
            out.append(jnp.where(v > 0, v, LEAK * v))
        return out

    loads[0].wait()
    loads[16].wait()

    def send_hidden(pieces):
        for side in range(2):

            @pl.when(sends[side])
            def _():
                for piece in pieces:
                    hid_copy(side, piece).start()

    for part, (first, end) in enumerate(PAIRS):
        for side in range(2):

            @pl.when(gets[side])
            def _():
                arrived(
                    raw.at[2 * side, :, pl.ds(0, 2 * (end - first) * 128)], lat_r.at[side, part]
                )

        for i in range(first, end):
            pair = jnp.concatenate([column(raw, i), column(raw, i + COLS // 2)], axis=1)
            folded = dot(pair, fold[:256])
            put(a1, 2 * i + 1, folded[:, :128])
            put(a1, 2 * i + 2, folded[:, 128:])
        if end == COLS // 2:
            close(a1)
        for j, v in zip(FIRST[part], convolved(wp1, a1, FIRST[part])):
            a2[1, :, (j + 1) * 128 : (j + 2) * 128] = v.astype(BF16)
        send_hidden((part, part + 1) if end == COLS // 2 else (part,))
        give_rims(part)

    def beside(now, c, planes):
        return now[pl.ds(pl.multiple_of(c * BLOCK + planes * FY, FY), BLOCK)]

    def laplace(now, blocks):
        centres = [now[rows(c)] for c in blocks]
        halves = [two(v) for v in centres]
        down = dot(
            along_y[...],
            jnp.concatenate([jnp.concatenate(h, axis=0) for h in halves], axis=1),
        )
        across = dot(
            jnp.concatenate([jnp.concatenate(h, axis=1) for h in halves], axis=0), along_x[...]
        )
        laps = []
        for i, (c, v) in enumerate(zip(blocks, centres)):
            lap = CENTRE * v + down[:, FX * i : FX * (i + 1)]
            lap = lap + across[BLOCK * i : BLOCK * (i + 1)]
            for k in range(1, 5):
                lap = lap + (SCALE * C[k]) * (beside(now, c, -k) + beside(now, c, k))
            laps.append(lap)
        return laps

    def advance(t, b, lap, v, before):
        pulse = jnp.where(linear == source_at - (b - 2) * (BLOCK * FX), wavelet[t - 1, shot], 0.0)
        return 2.0 * v - before + pace[rows(b)] * lap + pulse

    def weighted(t, b, lap):
        return adj[t - 1, own(b)].astype(F32) * lap

    def observe(t, b, new):
        hi, lo = two(new)
        got = dot(hot[b - 2], jnp.concatenate([hi, lo], axis=1))
        seen[t - 1] += got[:, :FX] + got[:, FX:]

    def finish(t, c, lap, now, before, new_f):
        new = advance(t, c, lap, now[rows(c)], before[rows(c)])
        new_f[(own if t == STEPS else rows)(c)] = new
        return new

    def step(t, blocks, now, before, new_f):
        for c, lap in zip(blocks, laplace(now, blocks)):
            finish(t, c, lap, now, before, new_f)
            corr[own(c)] += weighted(t, c, lap)

    for i in (5, 6, 7, 8, 9, 10, 11):
        loads[i].wait()
    source_at = (
        (sources[0, shot] - slab * FPS) * (FY * FX) + sources[1, shot] * FX + sources[2, shot]
    )
    linear = lax.broadcasted_iota(jnp.int32, (BLOCK, FX), 0) * FX + lax.broadcasted_iota(
        jnp.int32, (BLOCK, FX), 1
    )

    def first_laplace(blocks):
        for c, lap in zip(blocks, laplace(f1, blocks)):
            lap1[rows(c)] = lap
            corr[own(c)] = weighted(1, c, lap)

    give_rims(4)
    first_laplace((3, 4))

    def get_hidden(piece):
        for side in range(2):

            @pl.when(gets[side])
            def _():
                arrived(a2.at[2 * side, :, pl.ds(128, 4 * 128)], hid_r.at[side, piece])

    for part, columns in enumerate(SECOND):
        get_hidden(part)
        if part == len(SECOND) - 1:
            close(a2)
        for j, v in zip(columns, convolved(wp2, a2, columns)):
            v = v * head_col[...]
            logits[8 * j : 8 * j + 8] = jnp.sum(v.reshape(CH // 8, 8, 128), axis=0)
    total_logits = jnp.sum(logits[...].reshape(COLS, 8, 128), axis=1)
    wave_speed = 1.5 + 3.0 / (1.0 + jnp.exp(-total_logits))
    vel[...] = wave_speed.astype(BF16)

    def vel_copy(k, to_slab, slot, send, recv):
        return remote(vel, vels.at[slot], vel_s.at[send], vel_r.at[recv], to_slab * SHOTS + k)

    lends_low = (shot <= 2) & has_low
    lends_high = (shot >= SHOTS - 3) & has_high

    def vel_sends():
        for j in range(1, SHOTS):
            vel_copy(lax.rem(shot + j, SHOTS), slab, shot + 3, 0, 0).start()

        @pl.when(lends_low)
        def _():
            for k in range(SHOTS):
                vel_copy(k, slab - 1, lax.rem(shot, 3) + 11, 1, 2).start()

        @pl.when(lends_high)
        def _():
            for k in range(SHOTS):
                vel_copy(k, slab + 1, lax.rem(shot + 1, 3), 1, 1).start()

    def vel_gets():
        arrived(vels.at[pl.ds(0, SHOTS - 1)], vel_r.at[0])
        for side in range(2):

            @pl.when(rim_gets[side])
            def _():
                arrived(vels.at[pl.ds(0, 3)], vel_r.at[side + 1])

    def rec_copy(j):
        return remote(rec, recs.at[j], rec_s.at[0], rec_r.at[0], peer(j))

    vel_sends()
    vels[shot + 3] = vel[...]
    for side in range(2):
        edge, ext = ((2, 1), (5, 6))[side]

        @pl.when(rim_gets[side])
        def _():
            arrived(b1.at[pl.ds(0, BLOCK)], rim_r.at[side, 0])
            f1[rows((1, 6)[side])] = b1[rows((1, 6)[side])].astype(F32)

    first_laplace((2, 5))
    for side in range(2):
        ext, far = ((1, 0), (6, 7))[side]

        @pl.when(rim_gets[side])
        def _():
            arrived(b1.at[pl.ds(0, 2 * BLOCK)], rim_r.at[side, 1])
            f1[rows(far)] = b1[rows(far)].astype(F32)
            f0[rows(ext)] = halo0[side].astype(F32)
            lap1[rows(ext)] = laplace(f1, (ext,))[0]

    vel_gets()
    planes = []
    for i in range(2 * GROUP):
        plane = jnp.clip(slab * SHOTS - 3 + i, 0, n - 1)
        planes.append(vels[plane - slab * SHOTS + 3])
    wide = dot(jnp.concatenate(planes, axis=0), up_x[...])
    tall = []
    for g in range(2):
        part = wide[16 * GROUP * g : 16 * GROUP * (g + 1)]
        hi, lo = two(jnp.concatenate([part[:, :FX], part[:, FX:]], axis=0))
        both = dot(up_y[...], jnp.concatenate([hi, lo], axis=1))
        both = both[:, :FX] + both[:, FX:]
        tall += [both[FY * i : FY * (i + 1)] for i in range(GROUP)]
    for z in range(-4, FPS + 4):
        i = z // 2 + 3
        fine = 0.75 * tall[i] + 0.25 * tall[i + 1 if z % 2 else i - 1]
        at = z * FY + 2 * BLOCK
        if 0 <= z < FPS:
            speed[z * FY : (z + 1) * FY] = fine
        courant = COURANT * fine
        pace[at : at + FY] = courant * courant * (1.0 / SCALE)

    n1, n2 = jnp.where(has_low, 2, 5), jnp.where(has_low, 3, 4)
    g1, g2 = 7 - n1, 7 - n2
    far_too = has_low & has_high

    def second(c):
        finish(1, c, lap1[rows(c)], f1, f0, f2)

    for side in range(2):

        @pl.when(rim_gets[side])
        def _():
            second((1, 6)[side])

    for b in (2, 3, 4, 5):
        second(b)
    step(2, (n1, n2), f2, f1, f3)
    for c in (n1, n2):
        b3[rows(c)] = f3[rows(c)].astype(BF16)

    @pl.when(has_low)
    def _():
        rim_copy(1, 3).start()

    @pl.when(has_high & jnp.logical_not(has_low))
    def _():
        rim_copy(0, 3).start()

    step(2, (g1, g2), f2, f1, f3)

    @pl.when(far_too)
    def _():
        b3[4 * BLOCK : 6 * BLOCK] = f3[4 * BLOCK : 6 * BLOCK].astype(BF16)
        rim_copy(0, 3).start()

    for b in (2, 3, 4, 5):
        observe(1, b, f2[rows(b)])
        observe(2, b, f3[rows(b)])

    @pl.when(far_too)
    def _():
        rim_copy(1, 3).wait_recv()
        f3[6 * BLOCK :] = b3[6 * BLOCK :].astype(F32)
        finish(3, 6, laplace(f3, (6,))[0], f3, f2, f4)

    step(3, (g1, g2), f3, f2, f4)
    step(3, (n2,), f3, f2, f4)
    step(4, (g1, g2), f4, f3, final_out)
    for b in (g1, g2):
        observe(4, b, final_out[own(b)])
    for b in (g1, g2, n2):
        observe(3, b, f4[rows(b)])

    def collected(first):
        parts = []
        for t in (first, first + 1):
            parts += two(jnp.where(at_col, seen[t - 1], 0.0))
        wide = (8, 4 * FX)
        pick = lax.broadcasted_iota(jnp.int32, wide, 0) == first - 1 + lax.broadcasted_iota(
            jnp.int32, wide, 1
        ) // (2 * FX)
        line = dot(
            pick.astype(F32).astype(BF16), jnp.concatenate(parts, axis=1), ((1,), (1,))
        )
        rec[...] += line[:STEPS]

    collected(1)
    loads[13].wait()
    loads[14].wait()

    def raised(pair):
        at = pl.ds(pl.multiple_of(pair * 2 * BLOCK, 2 * BLOCK), 2 * BLOCK)
        fine = (2.0 * COURANT * COURANT / SCALE) * speed[at] * corr[at]
        return dot(up_zyt[pair], fine.astype(BF16))

    near_pair = jnp.where(has_low, 0, 1)
    tall = raised(1 - near_pair)
    @pl.when(has_low)
    def _():
        rim_copy(0, 3).wait_recv()

    @pl.when(has_high & jnp.logical_not(has_low))
    def _():
        rim_copy(1, 3).wait_recv()

    halo = pl.ds(pl.multiple_of(jnp.where(has_low, 0, 6 * BLOCK), 2 * BLOCK), 2 * BLOCK)
    ext = jnp.where(has_low, 1, 6)
    f3[halo] = b3[halo].astype(F32)
    lap_ext, lap = laplace(f3, (ext, n1))
    finish(3, ext, lap_ext, f3, f2, f4)
    finish(3, n1, lap, f3, f2, f4)
    corr[own(n1)] += weighted(3, n1, lap)
    step(4, (n1, n2), f4, f3, final_out)
    observe(3, n1, f4[rows(n1)])
    for b in (n1, n2):
        observe(4, b, final_out[own(b)])
    collected(3)
    tall = tall + raised(near_pair)
    half = tall.shape[0] // 2
    hi, lo = two(jnp.concatenate([tall[:half], tall[half:]], axis=1))
    narrow = dot(hi, up_xt[...]) + dot(lo, up_xt[...])
    gr[...] = narrow.reshape(SHOTS + 2, 16, FX)
    over_peers(lambda j: rec_copy(j).start())


    @pl.when(jnp.logical_not(has_low))
    def _():
        gr[1] += gr[0]

    @pl.when(jnp.logical_not(has_high))
    def _():
        gr[SHOTS] += gr[SHOTS + 1]

    def gr_copy(j):
        other = lax.rem(shot + j, SHOTS)
        return remote(
            gr.at[other + 1], grs.at[j], gr_s.at[0], gr_r.at[0], slab * SHOTS + other
        )

    def low_copy(slot):
        return remote(
            gr.at[0], grs.at[slot], gr_s.at[1], gr_r.at[1], lax.rem(slab * SHOTS - 1 + n, n)
        )

    def high_copy(slot):
        return remote(
            gr.at[SHOTS + 1],
            grs.at[slot],
            gr_s.at[2],
            gr_r.at[2],
            lax.rem((slab + 1) * SHOTS, n),
        )

    @pl.when(has_low)
    def _():
        low_copy(8 + shot).start()

    @pl.when(has_high)
    def _():
        high_copy(16 + shot).start()

    for j in range(1, SHOTS):
        gr_copy(j).start()


    recs[0] = rec[...]
    arrived(recs.at[pl.ds(1, n - 1)], rec_r.at[0])
    for s in range(SHOTS):

        def slab_term(k, acc):
            return acc + recs[lax.rem(me - (k * SHOTS + s) + n, n)]

        summed = lax.fori_loop(0, slabs, slab_term, jnp.zeros((STEPS, FX), F32))
        traces_out[s] = summed

    arrived(grs.at[pl.ds(1, SHOTS - 1)], gr_r.at[0])
    summed = gr[shot + 1]
    for j in range(1, SHOTS):
        summed = summed + grs[j]
    total[...] = summed

    @pl.when((shot == SHOTS - 1) & has_high)
    def _():
        arrived(grs.at[pl.ds(8, SHOTS)], gr_r.at[1])
        total[...] += jnp.sum(grs[8:16], axis=0)

    @pl.when((shot == 0) & has_low)
    def _():
        arrived(grs.at[pl.ds(16, SHOTS)], gr_r.at[2])
        total[...] += jnp.sum(grs[16:24], axis=0)

    gradient_out[...] = total[...]

    for side in range(2):

        @pl.when(sends[side])
        def _():
            departed(raw.at[0], lat_s.at[side])
            departed(a2.at[1, :, pl.ds(128, CELLS)], hid_s.at[side])

        @pl.when(rim_sends[side])
        def _():
            departed(b1.at[pl.ds(0, 3 * BLOCK)], rim_s.at[side, 0])
            departed(b3.at[pl.ds(0, 2 * BLOCK)], rim_s.at[side, 1])

    departed(vels.at[pl.ds(0, SHOTS - 1)], vel_s.at[0])

    @pl.when(lends_low | lends_high)
    def _():
        departed(vels.at[pl.ds(0, SHOTS)], vel_s.at[1])

    departed(recs.at[pl.ds(1, n - 1)], rec_s.at[0])
    departed(grs.at[pl.ds(1, SHOTS - 1)], gr_s.at[0])

    @pl.when(has_low)
    def _():
        departed(grs.at[0], gr_s.at[1])

    @pl.when(has_high)
    def _():
        departed(grs.at[0], gr_s.at[2])


def hand_over(a, b, c, x, y, z, sem):
    rows = FPS * FY // HALVES
    parts = [
        (a.at[pl.ds(i * rows, rows)], x.at[pl.ds(i * rows, rows)]) for i in range(HALVES)
    ]
    parts += [(b, y), (c, z)]
    copies = [pltpu.make_async_copy(src, dst, sem.at[i]) for i, (src, dst) in enumerate(parts)]
    for copy in copies:
        copy.start()
    for copy in copies:
        copy.wait()


def body(
    n,
    latent,
    conv1_weight,
    conv2_weight,
    head,
    p_prev,
    p_cur,
    adjoint,
    wavelet,
    sources,
    receivers,
):
    along_x, along_y, up_y, up_zyt, up_x, up_xt, fold = constants()
    vmem = pl.BlockSpec(memory_space=pltpu.VMEM)
    hbm = pl.BlockSpec(memory_space=pl.ANY)
    dma = pltpu.SemaphoreType.DMA
    final, traces, gradient = pl.pallas_call(
        functools.partial(kernel, n),
        out_shape=(
            pltpu.VMEM((FPS * FY, FX), F32),
            pltpu.VMEM((SHOTS, STEPS, 128), F32),
            pltpu.VMEM((16, FX), F32),
        ),
        in_specs=[hbm] * 17,
        out_specs=(vmem, vmem, vmem),
        scratch_shapes=[
            pltpu.VMEM((1, CH), BF16),
            pltpu.VMEM(conv1_weight.shape, BF16),
            pltpu.VMEM(conv2_weight.shape, BF16),
            pltpu.SMEM((STEPS, SHOTS), F32),
            pltpu.SMEM((3, SHOTS), jnp.int32),
            pltpu.VMEM((3, SHOTS, 128), jnp.int32),
            pltpu.VMEM(along_x.shape, BF16),
            pltpu.VMEM(along_y.shape, BF16),
            pltpu.VMEM(up_x.shape, BF16),
            pltpu.VMEM(up_xt.shape, BF16),
            pltpu.VMEM((WINDOW, FX), F32),
            pltpu.VMEM((CH, 128), F32),
            pltpu.VMEM((3, CH, CELLS), BF16),
            pltpu.VMEM(fold.shape, BF16),
            pltpu.VMEM((3, CH, (COLS + 2) * 128), BF16),
            pltpu.VMEM((3, CH, (COLS + 2) * 128), BF16),
            pltpu.VMEM((3 * CH, 9 * CH), BF16),
            pltpu.VMEM((3 * CH, 9 * CH), BF16),
            pltpu.VMEM((COLS * 8, 128), F32),
            pltpu.VMEM((16, FX), BF16),
            pltpu.VMEM((2 * GROUP, 16, FX), BF16),
            *[pltpu.VMEM((WINDOW, FX), F32)] * 5,
            *[pltpu.VMEM((WINDOW, FX), BF16)] * 2,
            pltpu.VMEM((STEPS, FPS * FY, FX), BF16),
            pltpu.VMEM(up_y.shape, BF16),
            pltpu.VMEM(up_zyt.shape, BF16),
            pltpu.VMEM((FPS * FY, FX), F32),
            pltpu.VMEM((FPS * FY, FX), F32),
            pltpu.VMEM((WINDOW, FX), F32),
            pltpu.VMEM((2, BLOCK, FX), BF16),
            pltpu.VMEM((2, BLOCK, FX), BF16),
            pltpu.VMEM((4, 128, BLOCK), BF16),
            pltpu.VMEM((STEPS, 128, FX), F32),
            pltpu.VMEM((STEPS, FX), F32),
            pltpu.VMEM((n, STEPS, FX), F32),
            pltpu.VMEM((SHOTS + 2, 16, FX), F32),
            pltpu.VMEM((3 * SHOTS, 16, FX), F32),
            pltpu.VMEM((16, FX), F32),
            dma((18,)),
            dma((2,)),
            dma((2, 4)),
            dma((2,)),
            dma((2, 4)),
            dma((2, 2)),
            dma((2, 3)),
            dma((2,)),
            dma((3,)),
            dma((1,)),
            dma((1,)),
            dma((3,)),
            dma((3,)),
        ],
        compiler_params=pltpu.CompilerParams(
            collective_id=0, has_side_effects=True, vmem_limit_bytes=VMEM_BYTES
        ),
    )(
        latent.reshape(CH, CELLS),
        conv1_weight,
        conv2_weight,
        head.reshape(1, CH),
        wavelet.T,
        sources.T,
        receivers.transpose(1, 0, 2),
        along_x,
        along_y,
        up_x,
        up_xt,
        p_prev.reshape(FPS * FY, FX),
        p_cur.reshape(FPS * FY, FX),
        adjoint.reshape(STEPS, FPS * FY, FX),
        up_y,
        up_zyt,
        fold,
    )
    final, traces, gradient = pl.pallas_call(
        hand_over,
        out_shape=(
            jax.ShapeDtypeStruct((FPS * FY, FX), F32),
            jax.ShapeDtypeStruct((SHOTS, STEPS, 128), F32),
            jax.ShapeDtypeStruct((16, FX), F32),
        ),
        in_specs=[vmem] * 3,
        out_specs=[hbm] * 3,
        scratch_shapes=[dma((HALVES + 2,))],
    )(*[pltpu.with_memory_space_constraint(v, pltpu.VMEM) for v in (final, traces, gradient)])
    return final.reshape(1, FPS, FY, FX), traces, gradient.reshape(1, CELLS)


def solution(mesh):
    in_specs = (
        P(None, ("groups", "slab"), None),
        P(),
        P(),
        P(),
        P(("groups", "slab"), None, None, None),
        P(("groups", "slab"), None, None, None),
        P(None, ("groups", "slab"), None, None, None),
        P("groups", None),
        P("groups", None),
        P("groups", None, None),
    )
    out_specs = (
        P(("groups", "slab"), None, None, None),
        P("groups", None, None),
        P(("groups", "slab"), None),
    )
    return jax.shard_map(
        functools.partial(body, mesh.shape["slab"]),
        mesh=mesh,
        in_specs=in_specs,
        out_specs=out_specs,
        check_vma=False,
    )
```

```python
import functools

import jax
import jax.numpy as jnp
import numpy as np
from jax import lax
from jax.experimental import pallas as pl
from jax.experimental.pallas import tpu as pltpu
from jax.sharding import PartitionSpec as P

CY = 32
CX = 64
CELLS = CY * CX
CH = 64
SHOTS = 8
STEPS = 4
FPS = 16
FY = 64
FX = 128
VMEM_BYTES = 60 * 2**20
WHATS = (0, 1, 2, 4, 5)
RIMS_AT = ((-1, 4,4,6,6), (-1, 4,6,7,7))
HALVES = 1
PAIRS = ((0, 3), (3, 5), (5, 7), (7, 8))
FIRST = ((1, 2, 3, 4), (5, 6, 7, 8), (9, 10, 11, 12), (13, 14, 15, 0))
PIECES = ((1, 5), (5, 9), (9, 13), (13, 16), (0, 1))
SECOND = ((2, 3), (4, 5, 6, 7), (8, 9, 10, 11), (12, 13, 14, 15, 0, 1))
COLS = CY // 2

C = (-205.0 / 72.0, 8.0 / 5.0, -1.0 / 5.0, 8.0 / 315.0, -1.0 / 560.0)
BLOCK = 4 * FY
OWN = 3
WINDOW = (2 * OWN + 4) * BLOCK
GROUP = 6
REACH = 5
SCALE = 5040.0
CENTRE = 3.0 * SCALE * C[0]
COURANT = 0.088
LEAK = 0.2
F32 = jnp.float32
BF16 = jnp.bfloat16


def near(i, j):
    k = abs(i - j)
    return SCALE * C[k] if 1 <= k <= 4 else 0.0


def banded(n):
    return np.array([[near(i, j) for j in range(n)] for i in range(n)])


def doubling(n):
    u = np.zeros((2 * n, n))
    for k in range(n):
        u[2 * k, k] += 0.75
        u[2 * k, max(k - 1, 0)] += 0.25
        u[2 * k + 1, k] += 0.75
        u[2 * k + 1, min(k + 1, n - 1)] += 0.25
    return u


def constants():
    along_x = np.concatenate([banded(FX)] * 2, axis=0)
    along_y = np.concatenate([np.kron(np.eye(4), banded(FY))] * 2, axis=1)
    depth = np.zeros((FPS, SHOTS + 2))
    for k in range(SHOTS):
        depth[2 * k, k + 1] = 0.75
        depth[2 * k, k] = 0.25
        depth[2 * k + 1, k + 1] = 0.75
        depth[2 * k + 1, k + 2] = 0.25
    rows = doubling(CY)
    each = np.eye(GROUP)
    up_y = np.concatenate(
        [np.kron(each, rows[:, : CY // 2]), np.kron(each, rows[:, CY // 2 :])], axis=1
    )
    down_zy = np.concatenate([np.kron(depth, rows[:, 0::2]), np.kron(depth, rows[:, 1::2])], axis=1).T
    eye = np.eye(CX)
    fold = np.zeros((4, 4))
    for i, o in ((0, 0), (1, 2), (2, 1), (3, 3)):
        fold[i, o] = 1
    fold = np.kron(fold, eye)
    up_x = np.kron(np.eye(2), doubling(CX).T)
    down_zy = np.stack(np.split(down_zy, 4, axis=1))
    out = (along_x, along_y, up_y, down_zy, up_x, up_x.T, fold)
    return [jnp.asarray(a.astype(jnp.bfloat16)) for a in out]


def dot(a, b, dims=((1,), (0,))):
    return lax.dot_general(a, b, (dims, ((), ())), preferred_element_type=F32)


def two(v):
    hi = v.astype(BF16)
    return hi, (v - hi.astype(F32)).astype(BF16)


def kernel(
    n,
    latent,
    w1_hbm,
    w2_hbm,
    head_hbm,
    wavelet_hbm,
    sources_hbm,
    receivers_hbm,
    along_x_hbm,
    along_y_hbm,
    up_x_hbm,
    up_xt_hbm,
    prev_hbm,
    cur_hbm,
    adj_hbm,
    up_y_hbm,
    up_zyt_hbm,
    fold_hbm,
    final_out,
    traces_out,
    gradient_out,
    head,
    w1,
    w2,
    wavelet,
    sources,
    receivers,
    along_x,
    along_y,
    up_x,
    up_xt,
    lap1,
    head_col,
    raw,
    fold,
    a1,
    a2,
    wp1,
    wp2,
    taps,
    logits,
    vel,
    vels,
    f0,
    f1,
    f2,
    f3,
    f4,
    f5,
    f6,
    b1,
    b3,
    adj,
    up_y,
    up_zyt,
    speed,
    corr,
    pace,
    edge0,
    halo0,
    hot,
    seen,
    rec,
    recs,
    gr,
    grs,
    total,
    local_sem,
    lat_s,
    lat_r,
    hid_s,
    hid_r,
    rim_s,
    rim_r,
    vel_s,
    vel_r,
    rec_s,
    rec_r,
    gr_s,
    gr_r,
):
    me = lax.axis_index("slab")
    shot = lax.rem(me, SHOTS)
    slab = me // SHOTS
    slabs = n // SHOTS
    has_low = slab > 0
    has_high = slab < slabs - 1

    sends = (me < n - 1, me > 0)
    gets = (me > 0, me < n - 1)
    inner = pl.ds(OWN * BLOCK, 4 * BLOCK)
    pairs = (
        (latent, raw.at[1]),
        (w1_hbm, w1),
        (cur_hbm, f1.at[inner]),
        (w2_hbm, w2),
        (receivers_hbm, receivers),
        (along_y_hbm, along_y),
        (along_x_hbm, along_x),
        (adj_hbm, adj),
        (up_x_hbm, up_x),
        (up_y_hbm, up_y),
        (wavelet_hbm, wavelet),
        (sources_hbm, sources),
        (prev_hbm, f0.at[inner]),
        (up_zyt_hbm, up_zyt),
        (up_xt_hbm, up_xt),
        (head_hbm, head),
        (fold_hbm, fold),
    )
    loads = [
        pltpu.make_async_copy(src, dst, local_sem.at[i]) for i, (src, dst) in enumerate(pairs)
    ]

    def remote(src, dst, send, recv, target):
        return pltpu.make_async_remote_copy(
            src_ref=src,
            dst_ref=dst,
            send_sem=send,
            recv_sem=recv,
            device_id={"slab": target},
            device_id_type=pl.DeviceIdType.MESH,
        )

    def peer(j):
        return lax.rem(me + j, n)

    barrier = pltpu.get_barrier_semaphore()

    def over_peers(what):
        def one(j, carry):
            what(j)
            return carry

        if n <= 16:
            for j in range(1, n):
                what(j)
        else:
            lax.fori_loop(1, n, one, 0)

    def greet(j):
        pl.semaphore_signal(
            barrier, inc=1, device_id={"slab": peer(j)}, device_id_type=pl.DeviceIdType.MESH
        )

    over_peers(greet)
    for load in loads:
        load.start()

    for a in (raw, a2):
        for side in range(2):

            @pl.when(jnp.logical_not(gets[side]))
            def _():
                a[2 * side] = jnp.zeros(a.shape[1:], BF16)

    pl.semaphore_wait(barrier, n - 1)

    def lat_copy(side, part, half):
        first, end = PAIRS[part]
        cols = pl.ds((first + half * COLS // 2) * 128, (end - first) * 128)
        return remote(
            latent.at[:, cols],
            raw.at[2 * side, :, cols],
            lat_s.at[side],
            lat_r.at[side, part],
            peer(1 if side == 0 else n - 1),
        )

    def arrived(ref, sem):
        remote(ref, ref, sem, sem, me).wait_recv()

    def departed(ref, sem):
        remote(ref, ref, sem, sem, me).wait_send()

    def hid_copy(side, piece):
        first, end = PIECES[piece]
        cols = pl.ds((first + 1) * 128, (end - first) * 128)
        return remote(
            a2.at[1, :, cols],
            a2.at[2 * side, :, cols],
            hid_s.at[side],
            hid_r.at[side, min(piece, 3)],
            peer(1 if side == 0 else n - 1),
        )

    def rim_copy(side, what):
        if what in (2, 5):
            src, dst = edge0.at[side, what // 3], halo0.at[side, what // 3]
        else:
            b, deep = {0: (b1, 0), 1: (b1, 1), 3: (b3, 1), 4: (b1, 2)}[what]
            block = (6 - deep, 3 + deep)[side]
            to = (2 - deep, 7 + deep)[side]
            src, dst = b.at[pl.ds(block * BLOCK, BLOCK)], b.at[pl.ds(to * BLOCK, BLOCK)]
        return remote(
            src,
            dst,
            rim_s.at[side, (0, 0, 0, 1, 2, 2)[what]],
            rim_r.at[side, (0, 1, 1, 2, 3, 3)[what]],
            peer(SHOTS if side == 0 else n - SHOTS),
        )

    rim_sends = (has_high, has_low)
    rim_gets = (has_low, has_high)

    def rows(b):
        return pl.ds(pl.multiple_of(b * BLOCK, BLOCK), BLOCK)

    def own(b):
        return pl.ds(pl.multiple_of((b - OWN) * BLOCK, BLOCK), BLOCK)

    for part in range(len(PAIRS)):
        for side in range(2):

            @pl.when(sends[side])
            def _():
                lat_copy(side, part, 0).start()
                lat_copy(side, part, 1).start()

    loads[1].wait()
    loads[3].wait()
    for w, packed in ((w1, wp1), (w2, wp2)):
        for tap in range(9):
            packed[tap * CH : (tap + 1) * CH] = jnp.concatenate(
                [w[dz * 9 + tap] for dz in range(3)], axis=1
            )

    for side in range(2):
        ext = (2, 7)[side]

        @pl.when(jnp.logical_not(rim_gets[side]))
        def _():
            for f in (f1, f2, f3):
                f[ext * BLOCK : (ext + 1) * BLOCK] = jnp.zeros((BLOCK, FX), F32)

    for f, empty in ((f3, (1, 8)), (f4, (2, 7))):
        for b in empty:
            f[rows(b)] = jnp.zeros((BLOCK, FX), F32)

    for f in (f5, f6):
        f[...] = jnp.zeros(f.shape, F32)

    loads[2].wait()
    loads[12].wait()
    b1[inner] = f1[inner].astype(BF16)
    for side in range(2):
        for deep in range(2):
            edge0[side, deep] = f0[rows((6 - deep, 3 + deep)[side])].astype(BF16)

    middle = (slab == 0) == (shot >= SHOTS // 2)

    def give_rims(at):
        for times, mine in zip(RIMS_AT, (middle, jnp.logical_not(middle))):
            whats = [what for what, t in zip(WHATS, times) if t == at]
            for side in range(2):
                if whats:

                    @pl.when(rim_sends[side] & mine)
                    def _():
                        for what in whats:
                            rim_copy(side, what).start()

    give_rims(-1)
    loads[4].wait()
    loads[15].wait()
    station = receivers[:, shot]
    same = lax.broadcasted_iota(jnp.int32, (128, 128), 0) == lax.broadcasted_iota(
        jnp.int32, (128, 128), 1
    )

    def upright(v):
        return jnp.sum(
            jnp.where(same, jnp.broadcast_to(v.astype(F32), (128, 128)), 0.0), axis=1, keepdims=True
        ).astype(jnp.int32)

    station_row = upright((station[0:1] - slab * FPS) * FY + station[1:2])
    station_col = upright(station[2:3])
    row = lax.broadcasted_iota(jnp.int32, (128, BLOCK), 1)
    for b in range(4):
        hot[b] = (row + b * BLOCK == station_row).astype(F32).astype(BF16)
    at_col = lax.broadcasted_iota(jnp.int32, (128, FX), 1) == station_col
    seen[...] = jnp.zeros(seen.shape, F32)
    rec[...] = jnp.zeros((STEPS, FX), F32)

    square = (CH, CH)
    diagonal = lax.broadcasted_iota(jnp.int32, square, 0) == lax.broadcasted_iota(
        jnp.int32, square, 1
    )
    spread = jnp.broadcast_to(head[...].astype(F32), square)
    head_col[...] = jnp.broadcast_to(
        jnp.sum(jnp.where(diagonal, spread, 0.0), axis=1, keepdims=True), (CH, 128)
    )

    lane = lax.broadcasted_iota(jnp.int32, (1, 128), 1)
    keep_left = lax.rem(lane, CX) > 0
    keep_right = lax.rem(lane, CX) < CX - 1

    def column(a, c):
        return a[:, :, c * 128 : (c + 1) * 128].reshape(3 * CH, 128)

    def put(a, c, v):
        a[:, :, c * 128 : (c + 1) * 128] = v.astype(BF16).reshape(3, CH, 128)

    low_half = lane < CX

    def spread(packed, a, columns):
        block = jnp.concatenate([column(a, j + 1) for j in columns], axis=1)
        got = dot(packed[...], block)
        for i, j in enumerate(columns):
            taps[j] = got[:, i * 128 : (i + 1) * 128].reshape(9, CH, 128)

    def gathered(j):
        sums = []
        for dx in range(3):
            v = taps[j, 3 + dx]
            if j > 0:
                v = v + taps[j - 1, dx]
            else:
                v = v + jnp.where(low_half, 0.0, pltpu.roll(taps[COLS - 1, dx], CX, 1))
            if j < COLS - 1:
                v = v + taps[j + 1, 6 + dx]
            else:
                v = v + jnp.where(low_half, pltpu.roll(taps[0, 6 + dx], CX, 1), 0.0)
            sums.append(v)
        v = (
            sums[1]
            + jnp.where(keep_left, pltpu.roll(sums[0], 1, 1), 0.0)
            + jnp.where(keep_right, pltpu.roll(sums[2], 127, 1), 0.0)
        )
        return jnp.where(v > 0, v, LEAK * v)

    loads[0].wait()
    loads[16].wait()

    def send_hidden(pieces):
        for side in range(2):

            @pl.when(sends[side])
            def _():
                for piece in pieces:
                    hid_copy(side, piece).start()

    for part, (first, end) in enumerate(PAIRS):
        for side in range(2):

            @pl.when(gets[side])
            def _():
                arrived(
                    raw.at[2 * side, :, pl.ds(0, 2 * (end - first) * 128)], lat_r.at[side, part]
                )

        for i in range(first, end):
            pair = jnp.concatenate([column(raw, i), column(raw, i + COLS // 2)], axis=1)
            folded = dot(pair, fold[...])
            put(a1, 2 * i + 1, folded[:, :128])
            put(a1, 2 * i + 2, folded[:, 128:])
        spread(wp1, a1, range(2 * first, 2 * end))
        for j in FIRST[part]:
            a2[1, :, (j + 1) * 128 : (j + 2) * 128] = gathered(j).astype(BF16)
        send_hidden((part, part + 1) if end == COLS // 2 else (part,))
        give_rims(part)

    def beside(now, c, planes):
        return now[pl.ds(pl.multiple_of(c * BLOCK + planes * FY, FY), BLOCK)]

    def in_depth(now, c):
        lap = (SCALE * C[1]) * (beside(now, c, -1) + beside(now, c, 1))
        for k in range(2, 5):
            lap = lap + (SCALE * C[k]) * (beside(now, c, -k) + beside(now, c, k))
        return lap

    def laplace(now, blocks):
        centres = [now[rows(c)] for c in blocks]
        halves = [two(v) for v in centres]
        down = dot(
            along_y[...],
            jnp.concatenate([jnp.concatenate(h, axis=0) for h in halves], axis=1),
        )
        across = dot(
            jnp.concatenate([jnp.concatenate(h, axis=1) for h in halves], axis=0), along_x[...]
        )
        laps = []
        for i, (c, v) in enumerate(zip(blocks, centres)):
            lap = CENTRE * v + down[:, FX * i : FX * (i + 1)]
            lap = lap + across[BLOCK * i : BLOCK * (i + 1)]
            laps.append(lap + in_depth(now, c))
        return laps

    def advance(t, b, lap, v, before):
        pulse = jnp.where(linear == source_at - (b - OWN) * (BLOCK * FX), wavelet[t - 1, shot], 0.0)
        return 2.0 * v - before + pace[rows(b)] * lap + pulse

    def weighted(t, b, lap):
        return adj[t - 1, own(b)].astype(F32) * lap

    def observe(t, b, new):
        hi, lo = two(new)
        got = dot(hot[b - OWN], jnp.concatenate([hi, lo], axis=1))
        seen[t - 1] += got[:, :FX] + got[:, FX:]

    def finish(t, c, lap, now, before, new_f):
        new = advance(t, c, lap, now[rows(c)], before[rows(c)])
        new_f[(own if t == STEPS else rows)(c)] = new
        return new

    def step(t, blocks, now, before, new_f):
        for c, lap in zip(blocks, laplace(now, blocks)):
            finish(t, c, lap, now, before, new_f)
            corr[own(c)] += weighted(t, c, lap)

    for i in (5, 6, 7, 8, 9, 10, 11):
        loads[i].wait()
    source_at = (
        (sources[0, shot] - slab * FPS) * (FY * FX) + sources[1, shot] * FX + sources[2, shot]
    )
    linear = lax.broadcasted_iota(jnp.int32, (BLOCK, FX), 0) * FX + lax.broadcasted_iota(
        jnp.int32, (BLOCK, FX), 1
    )

    def first_laplace(blocks):
        for c, lap in zip(blocks, laplace(f1, blocks)):
            lap1[rows(c)] = lap
            corr[own(c)] = weighted(1, c, lap)

    give_rims(4)
    first_laplace((4, 5))

    def get_hidden(piece):
        for side in range(2):

            @pl.when(gets[side])
            def _():
                arrived(a2.at[2 * side, :, pl.ds(128, 4 * 128)], hid_r.at[side, piece])

    for part, columns in enumerate(SECOND):
        get_hidden(part)
        spread(wp2, a2, FIRST[part])
        for j in columns:
            v = gathered(j) * head_col[...]
            logits[8 * j : 8 * j + 8] = jnp.sum(v.reshape(CH // 8, 8, 128), axis=0)
    give_rims(5)
    total_logits = jnp.sum(logits[...].reshape(COLS, 8, 128), axis=1)
    wave_speed = 1.5 + 3.0 / (1.0 + jnp.exp(-total_logits))
    vel[...] = wave_speed.astype(BF16)

    def vel_copy(k, to_slab, slot, send, recv):
        return remote(vel, vels.at[slot], vel_s.at[send], vel_r.at[recv], to_slab * SHOTS + k)

    lends_low = (shot < REACH) & has_low
    lends_high = (shot >= SHOTS - REACH) & has_high

    def vel_sends():
        for j in range(1, SHOTS):
            vel_copy(lax.rem(shot + j, SHOTS), slab, shot + REACH, 0, 0).start()

        @pl.when(lends_low)
        def _():
            for k in range(SHOTS):
                vel_copy(k, slab - 1, lax.rem(shot, REACH) + SHOTS + REACH, 1, 2).start()

        @pl.when(lends_high)
        def _():
            for k in range(SHOTS):
                vel_copy(k, slab + 1, lax.rem(shot + 2, REACH), 2, 1).start()

    def vel_gets():
        arrived(vels.at[pl.ds(0, SHOTS - 1)], vel_r.at[0])
        for side in range(2):

            @pl.when(rim_gets[side])
            def _():
                arrived(vels.at[pl.ds(0, REACH)], vel_r.at[side + 1])

    def rec_copy(j):
        return remote(rec, recs.at[j], rec_s.at[0], rec_r.at[0], peer(j))

    vel_sends()
    vels[shot + REACH] = vel[...]
    give_rims(6)
    for side in range(2):
        @pl.when(rim_gets[side])
        def _():
            ext = (2, 7)[side]
            arrived(b1.at[pl.ds(0, BLOCK)], rim_r.at[side, 0])
            f1[rows(ext)] = b1[rows(ext)].astype(F32)

    first_laplace((3, 6))
    vel_gets()
    give_rims(7)
    planes = []
    for i in range(3 * GROUP):
        plane = jnp.clip(slab * SHOTS - REACH + i, 0, n - 1)
        planes.append(vels[plane - slab * SHOTS + REACH])
    wide = dot(jnp.concatenate(planes, axis=0), up_x[...])
    tall = []
    for g in range(3):
        part = wide[16 * GROUP * g : 16 * GROUP * (g + 1)]
        hi, lo = two(jnp.concatenate([part[:, :FX], part[:, FX:]], axis=0))
        both = dot(up_y[...], jnp.concatenate([hi, lo], axis=1))
        both = both[:, :FX] + both[:, FX:]
        tall += [both[FY * i : FY * (i + 1)] for i in range(GROUP)]
    for z in range(-8, FPS + 8):
        i = z // 2 + REACH
        fine = 0.75 * tall[i] + 0.25 * tall[i + 1 if z % 2 else i - 1]
        at = z * FY + OWN * BLOCK
        if 0 <= z < FPS:
            speed[z * FY : (z + 1) * FY] = fine
        courant = COURANT * fine
        pace[at : at + FY] = courant * courant * (1.0 / SCALE)

    n1, n2 = jnp.where(has_low, 3, 6), jnp.where(has_low, 4, 5)
    g1, g2 = 9 - n1, 9 - n2
    far_too = has_low & has_high

    def second(c):
        finish(1, c, lap1[rows(c)], f1, f0, f2)

    for b in (3, 4, 5, 6):
        second(b)
    step(2, (n2, g2), f2, f1, f3)
    for c in (4, 5):
        b3[rows(c)] = f3[rows(c)].astype(BF16)
    for side in range(2):

        @pl.when(rim_sends[side])
        def _():
            rim_copy(side, 3).start()

    def deeper(side):
        ext, far, last = ((2, 1, 0), (7, 8, 9))[side]
        arrived(b1.at[pl.ds(0, 2 * BLOCK)], rim_r.at[side, 1])
        arrived(b1.at[pl.ds(0, 2 * BLOCK)], rim_r.at[side, 3])
        for c in (far, last):
            f1[rows(c)] = b1[rows(c)].astype(F32)
        for i, c in enumerate((ext, far)):
            f0[rows(c)] = halo0[side, i].astype(F32)
        for c, lap in zip((ext, far), laplace(f1, (ext, far))):
            finish(1, c, lap, f1, f0, f2)
        finish(2, ext, laplace(f2, (ext,))[0], f2, f1, f3)

    give_rims(8)
    @pl.when(far_too)
    def _():
        deeper(1)

    step(2, (g1,), f2, f1, f3)
    def collected(first, last):
        parts = []
        for t in range(first, last + 1):
            parts += two(jnp.where(at_col, seen[t - 1], 0.0))
        wide = (8, (last - first + 1) * 2 * FX)
        pick = lax.broadcasted_iota(jnp.int32, wide, 0) == first - 1 + lax.broadcasted_iota(
            jnp.int32, wide, 1
        ) // (2 * FX)
        line = dot(
            pick.astype(F32).astype(BF16), jnp.concatenate(parts, axis=1), ((1,), (1,))
        )
        rec[...] += line[:STEPS]

    for b in (3, 4, 5, 6):
        observe(1, b, f2[rows(b)])
    for b in (g1, g2, n2):
        observe(2, b, f3[rows(b)])
    collected(1, 1)

    @pl.when(far_too)
    def _():
        rim_copy(1, 3).wait_recv()
        f3[rows(8)] = b3[rows(8)].astype(F32)
        finish(3, 7, laplace(f3, (7,))[0], f3, f2, f4)

    step(3, (g1, g2), f3, f2, f4)
    step(4, (g1,), f4, f3, final_out)
    for b in (g1, g2):
        observe(3, b, f4[rows(b)])
    observe(4, g1, final_out[own(g1)])
    loads[13].wait()
    loads[14].wait()

    def raised(c):
        fine = (2.0 * COURANT * COURANT / SCALE) * speed[own(c)] * corr[own(c)]
        return dot(up_zyt[c - OWN], fine.astype(BF16))

    ext, far = jnp.where(has_low, 2, 7), jnp.where(has_low, 1, 8)
    pl.when(has_low)(lambda: deeper(0))
    pl.when(has_high & jnp.logical_not(has_low))(lambda: deeper(1))
    step(2, (n1,), f2, f1, f3)
    step(3, (n2, n1), f3, f2, f4)
    step(4, (g2, n2), f4, f3, final_out)
    lap1[rows(ext)] = laplace(f3, (ext,))[0]
    lap1[rows(n1)] = laplace(f4, (n1,))[0]
    observe(2, n1, f3[rows(n1)])
    for b in (n2, n1):
        observe(3, b, f4[rows(b)])
    for b in (g2, n2):
        observe(4, b, final_out[own(b)])
    collected(2, 3)
    tall = raised(g1) + raised(g2) + raised(n2)
    @pl.when(has_low)
    def _():
        rim_copy(0, 3).wait_recv()

    @pl.when(has_high & jnp.logical_not(has_low))
    def _():
        rim_copy(1, 3).wait_recv()

    f5[rows(far)] = b3[rows(far)].astype(F32)
    lap = lap1[rows(ext)] + in_depth(f5, ext)
    f6[rows(ext)] = advance(3, ext, lap, f3[rows(ext)], f2[rows(ext)])
    lap = lap1[rows(n1)] + in_depth(f6, n1)
    last = finish(4, n1, lap, f4, f3, final_out)
    corr[own(n1)] += weighted(4, n1, lap)
    observe(4, n1, last)
    collected(4, 4)
    tall = tall + raised(n1)
    half = tall.shape[0] // 2
    hi, lo = two(jnp.concatenate([tall[:half], tall[half:]], axis=1))
    narrow = dot(hi, up_xt[...]) + dot(lo, up_xt[...])
    gr[...] = narrow.reshape(SHOTS + 2, 16, FX)
    over_peers(lambda j: rec_copy(j).start())


    @pl.when(jnp.logical_not(has_low))
    def _():
        gr[1] += gr[0]

    @pl.when(jnp.logical_not(has_high))
    def _():
        gr[SHOTS] += gr[SHOTS + 1]

    def gr_copy(j):
        other = lax.rem(shot + j, SHOTS)
        return remote(
            gr.at[other + 1], grs.at[j], gr_s.at[0], gr_r.at[0], slab * SHOTS + other
        )

    def low_copy(slot):
        return remote(
            gr.at[0], grs.at[slot], gr_s.at[1], gr_r.at[1], lax.rem(slab * SHOTS - 1 + n, n)
        )

    def high_copy(slot):
        return remote(
            gr.at[SHOTS + 1],
            grs.at[slot],
            gr_s.at[2],
            gr_r.at[2],
            lax.rem((slab + 1) * SHOTS, n),
        )

    @pl.when(has_low)
    def _():
        low_copy(8 + shot).start()

    @pl.when(has_high)
    def _():
        high_copy(16 + shot).start()

    for j in range(1, SHOTS):
        gr_copy(j).start()


    recs[0] = rec[...]
    arrived(recs.at[pl.ds(1, n - 1)], rec_r.at[0])
    for s in range(SHOTS):

        def slab_term(k, acc):
            return acc + recs[lax.rem(me - (k * SHOTS + s) + n, n)]

        summed = lax.fori_loop(0, slabs, slab_term, jnp.zeros((STEPS, FX), F32))
        traces_out[s] = summed

    arrived(grs.at[pl.ds(1, SHOTS - 1)], gr_r.at[0])
    summed = gr[shot + 1]
    for j in range(1, SHOTS):
        summed = summed + grs[j]
    total[...] = summed

    @pl.when((shot == SHOTS - 1) & has_high)
    def _():
        arrived(grs.at[pl.ds(8, SHOTS)], gr_r.at[1])
        total[...] += jnp.sum(grs[8:16], axis=0)

    @pl.when((shot == 0) & has_low)
    def _():
        arrived(grs.at[pl.ds(16, SHOTS)], gr_r.at[2])
        total[...] += jnp.sum(grs[16:24], axis=0)

    gradient_out[...] = total[...]

    for side in range(2):

        @pl.when(sends[side])
        def _():
            departed(raw.at[0], lat_s.at[side])
            departed(a2.at[1, :, pl.ds(128, CELLS)], hid_s.at[side])

        @pl.when(rim_sends[side])
        def _():
            departed(b1.at[pl.ds(0, 3 * BLOCK)], rim_s.at[side, 0])
            departed(b3.at[pl.ds(0, BLOCK)], rim_s.at[side, 1])
            departed(b1.at[pl.ds(0, 2 * BLOCK)], rim_s.at[side, 2])

    departed(vels.at[pl.ds(0, SHOTS - 1)], vel_s.at[0])

    for lends, sem in ((lends_low, 1), (lends_high, 2)):

        @pl.when(lends)
        def _():
            departed(vels.at[pl.ds(0, SHOTS)], vel_s.at[sem])

    departed(recs.at[pl.ds(1, n - 1)], rec_s.at[0])
    departed(grs.at[pl.ds(1, SHOTS - 1)], gr_s.at[0])

    @pl.when(has_low)
    def _():
        departed(grs.at[0], gr_s.at[1])

    @pl.when(has_high)
    def _():
        departed(grs.at[0], gr_s.at[2])


def hand_over(a, b, c, x, y, z, sem):
    rows = FPS * FY // HALVES
    parts = [
        (a.at[pl.ds(i * rows, rows)], x.at[pl.ds(i * rows, rows)]) for i in range(HALVES)
    ]
    parts += [(b, y), (c, z)]
    copies = [pltpu.make_async_copy(src, dst, sem.at[i]) for i, (src, dst) in enumerate(parts)]
    for copy in copies:
        copy.start()
    for copy in copies:
        copy.wait()


def body(
    n,
    latent,
    conv1_weight,
    conv2_weight,
    head,
    p_prev,
    p_cur,
    adjoint,
    wavelet,
    sources,
    receivers,
):
    along_x, along_y, up_y, up_zyt, up_x, up_xt, fold = constants()
    vmem = pl.BlockSpec(memory_space=pltpu.VMEM)
    hbm = pl.BlockSpec(memory_space=pl.ANY)
    dma = pltpu.SemaphoreType.DMA
    final, traces, gradient = pl.pallas_call(
        functools.partial(kernel, n),
        out_shape=(
            pltpu.VMEM((FPS * FY, FX), F32),
            pltpu.VMEM((SHOTS, STEPS, 128), F32),
            pltpu.VMEM((16, FX), F32),
        ),
        in_specs=[hbm] * 17,
        out_specs=(vmem, vmem, vmem),
        scratch_shapes=[
            pltpu.VMEM((1, CH), BF16),
            pltpu.VMEM(conv1_weight.shape, BF16),
            pltpu.VMEM(conv2_weight.shape, BF16),
            pltpu.SMEM((STEPS, SHOTS), F32),
            pltpu.SMEM((3, SHOTS), jnp.int32),
            pltpu.VMEM((3, SHOTS, 128), jnp.int32),
            pltpu.VMEM(along_x.shape, BF16),
            pltpu.VMEM(along_y.shape, BF16),
            pltpu.VMEM(up_x.shape, BF16),
            pltpu.VMEM(up_xt.shape, BF16),
            pltpu.VMEM((WINDOW, FX), F32),
            pltpu.VMEM((CH, 128), F32),
            pltpu.VMEM((3, CH, CELLS), BF16),
            pltpu.VMEM(fold.shape, BF16),
            pltpu.VMEM((3, CH, (COLS + 2) * 128), BF16),
            pltpu.VMEM((3, CH, (COLS + 2) * 128), BF16),
            pltpu.VMEM((9 * CH, 3 * CH), BF16),
            pltpu.VMEM((9 * CH, 3 * CH), BF16),
            pltpu.VMEM((COLS, 9, CH, 128), F32),
            pltpu.VMEM((COLS * 8, 128), F32),
            pltpu.VMEM((16, FX), BF16),
            pltpu.VMEM((3 * GROUP, 16, FX), BF16),
            *[pltpu.VMEM((WINDOW, FX), F32)] * 7,
            *[pltpu.VMEM((WINDOW, FX), BF16)] * 2,
            pltpu.VMEM((STEPS, FPS * FY, FX), BF16),
            pltpu.VMEM(up_y.shape, BF16),
            pltpu.VMEM(up_zyt.shape, BF16),
            pltpu.VMEM((FPS * FY, FX), F32),
            pltpu.VMEM((FPS * FY, FX), F32),
            pltpu.VMEM((WINDOW, FX), F32),
            pltpu.VMEM((2, 2, BLOCK, FX), BF16),
            pltpu.VMEM((2, 2, BLOCK, FX), BF16),
            pltpu.VMEM((4, 128, BLOCK), BF16),
            pltpu.VMEM((STEPS, 128, FX), F32),
            pltpu.VMEM((STEPS, FX), F32),
            pltpu.VMEM((n, STEPS, FX), F32),
            pltpu.VMEM((SHOTS + 2, 16, FX), F32),
            pltpu.VMEM((3 * SHOTS, 16, FX), F32),
            pltpu.VMEM((16, FX), F32),
            dma((18,)),
            dma((2,)),
            dma((2, 4)),
            dma((2,)),
            dma((2, 4)),
            dma((2, 3)),
            dma((2, 4)),
            dma((3,)),
            dma((3,)),
            dma((1,)),
            dma((1,)),
            dma((3,)),
            dma((3,)),
        ],
        compiler_params=pltpu.CompilerParams(
            collective_id=0, has_side_effects=True, vmem_limit_bytes=VMEM_BYTES
        ),
    )(
        latent.reshape(CH, CELLS),
        conv1_weight,
        conv2_weight,
        head.reshape(1, CH),
        wavelet.T,
        sources.T,
        receivers.transpose(1, 0, 2),
        along_x,
        along_y,
        up_x,
        up_xt,
        p_prev.reshape(FPS * FY, FX),
        p_cur.reshape(FPS * FY, FX),
        adjoint.reshape(STEPS, FPS * FY, FX),
        up_y,
        up_zyt,
        fold,
    )
    final, traces, gradient = pl.pallas_call(
        hand_over,
        out_shape=(
            jax.ShapeDtypeStruct((FPS * FY, FX), F32),
            jax.ShapeDtypeStruct((SHOTS, STEPS, 128), F32),
            jax.ShapeDtypeStruct((16, FX), F32),
        ),
        in_specs=[vmem] * 3,
        out_specs=[hbm] * 3,
        scratch_shapes=[dma((HALVES + 2,))],
    )(*[pltpu.with_memory_space_constraint(v, pltpu.VMEM) for v in (final, traces, gradient)])
    return final.reshape(1, FPS, FY, FX), traces, gradient.reshape(1, CELLS)


def solution(mesh):
    in_specs = (
        P(None, ("groups", "slab"), None),
        P(),
        P(),
        P(),
        P(("groups", "slab"), None, None, None),
        P(("groups", "slab"), None, None, None),
        P(None, ("groups", "slab"), None, None, None),
        P("groups", None),
        P("groups", None),
        P("groups", None, None),
    )
    out_specs = (
        P(("groups", "slab"), None, None, None),
        P("groups", None, None),
        P(("groups", "slab"), None),
    )
    return jax.shard_map(
        functools.partial(body, mesh.shape["slab"]),
        mesh=mesh,
        in_specs=in_specs,
        out_specs=out_specs,
        check_vma=False,
    )
```

```python
import functools

import jax
import jax.numpy as jnp
import numpy as np
from jax import lax
from jax.experimental import pallas as pl
from jax.experimental.pallas import tpu as pltpu
from jax.sharding import PartitionSpec as P

CY = 32
CX = 64
CELLS = CY * CX
CH = 64
SHOTS = 8
STEPS = 4
FPS = 16
FY = 64
FX = 128
VMEM_BYTES = 60 * 2**20
WHATS = (0, 1, 2, 4, 5)
RIMS_AT = ((-1, 4,4,6,6), (-1, 4,6,7,7))
HALVES = 1
PAIRS = ((0, 3), (3, 5), (5, 7), (7, 8))
FIRST = ((1, 2, 3, 4), (5, 6, 7, 8), (9, 10, 11, 12), (13, 14, 15, 0))
PIECES = ((1, 5), (5, 9), (9, 13), (13, 16), (0, 1))
SECOND = ((2, 3), (4, 5, 6, 7), (8, 9, 10, 11), (12, 13, 14, 15, 0, 1))
COLS = CY // 2

C = (-205.0 / 72.0, 8.0 / 5.0, -1.0 / 5.0, 8.0 / 315.0, -1.0 / 560.0)
BLOCK = 4 * FY
OWN = 3
WINDOW = (2 * OWN + 4) * BLOCK
GROUP = 6
REACH = 5
SCALE = 5040.0
CENTRE = 3.0 * SCALE * C[0]
COURANT = 0.088
LEAK = 0.2
F32 = jnp.float32
BF16 = jnp.bfloat16


def near(i, j):
    k = abs(i - j)
    return SCALE * C[k] if 1 <= k <= 4 else 0.0


def banded(n):
    return np.array([[near(i, j) for j in range(n)] for i in range(n)])


def doubling(n):
    u = np.zeros((2 * n, n))
    for k in range(n):
        u[2 * k, k] += 0.75
        u[2 * k, max(k - 1, 0)] += 0.25
        u[2 * k + 1, k] += 0.75
        u[2 * k + 1, min(k + 1, n - 1)] += 0.25
    return u


def constants():
    along_x = np.concatenate([banded(FX)] * 2, axis=0)
    along_y = np.concatenate([np.kron(np.eye(4), banded(FY))] * 2, axis=1)
    depth = np.zeros((FPS, SHOTS + 2))
    for k in range(SHOTS):
        depth[2 * k, k + 1] = 0.75
        depth[2 * k, k] = 0.25
        depth[2 * k + 1, k + 1] = 0.75
        depth[2 * k + 1, k + 2] = 0.25
    rows = doubling(CY)
    each = np.eye(GROUP)
    up_y = np.concatenate(
        [np.kron(each, rows[:, : CY // 2]), np.kron(each, rows[:, CY // 2 :])], axis=1
    )
    down_zy = np.concatenate([np.kron(depth, rows[:, 0::2]), np.kron(depth, rows[:, 1::2])], axis=1).T
    eye = np.eye(CX)
    fold = np.zeros((4, 4))
    for i, o in ((0, 0), (1, 2), (2, 1), (3, 3)):
        fold[i, o] = 1
    fold = np.kron(fold, eye)
    up_x = np.kron(np.eye(2), doubling(CX).T)
    down_zy = np.stack(np.split(down_zy, 4, axis=1))
    out = (along_x, along_y, up_y, down_zy, up_x, up_x.T, fold)
    return [jnp.asarray(a.astype(jnp.bfloat16)) for a in out]


def dot(a, b, dims=((1,), (0,))):
    return lax.dot_general(a, b, (dims, ((), ())), preferred_element_type=F32)


def two(v):
    hi = v.astype(BF16)
    return hi, (v - hi.astype(F32)).astype(BF16)


def kernel(
    n,
    latent,
    w1_hbm,
    w2_hbm,
    head_hbm,
    wavelet_hbm,
    sources_hbm,
    receivers_hbm,
    along_x_hbm,
    along_y_hbm,
    up_x_hbm,
    up_xt_hbm,
    prev_hbm,
    cur_hbm,
    adj_hbm,
    up_y_hbm,
    up_zyt_hbm,
    fold_hbm,
    final_out,
    traces_out,
    gradient_out,
    head,
    w1,
    w2,
    wavelet,
    sources,
    receivers,
    along_x,
    along_y,
    up_x,
    up_xt,
    lap1,
    head_col,
    raw,
    fold,
    a1,
    a2,
    wp1,
    wp2,
    taps,
    logits,
    vel,
    vels,
    f0,
    f1,
    f2,
    f3,
    f4,
    f5,
    f6,
    b1,
    b3,
    adj,
    up_y,
    up_zyt,
    speed,
    corr,
    pace,
    edge0,
    halo0,
    hot,
    seen,
    rec,
    recs,
    gr,
    grs,
    total,
    local_sem,
    lat_s,
    lat_r,
    hid_s,
    hid_r,
    rim_s,
    rim_r,
    vel_s,
    vel_r,
    rec_s,
    rec_r,
    gr_s,
    gr_r,
):
    me = lax.axis_index("slab")
    shot = lax.rem(me, SHOTS)
    slab = me // SHOTS
    slabs = n // SHOTS
    has_low = slab > 0
    has_high = slab < slabs - 1

    sends = (me < n - 1, me > 0)
    gets = (me > 0, me < n - 1)
    inner = pl.ds(OWN * BLOCK, 4 * BLOCK)
    pairs = (
        (latent, raw.at[1]),
        (w1_hbm, w1),
        (cur_hbm, f1.at[inner]),
        (w2_hbm, w2),
        (receivers_hbm, receivers),
        (along_y_hbm, along_y),
        (along_x_hbm, along_x),
        (adj_hbm, adj),
        (up_x_hbm, up_x),
        (up_y_hbm, up_y),
        (wavelet_hbm, wavelet),
        (sources_hbm, sources),
        (prev_hbm, f0.at[inner]),
        (up_zyt_hbm, up_zyt),
        (up_xt_hbm, up_xt),
        (head_hbm, head),
        (fold_hbm, fold),
    )
    loads = [
        pltpu.make_async_copy(src, dst, local_sem.at[i]) for i, (src, dst) in enumerate(pairs)
    ]

    def remote(src, dst, send, recv, target):
        return pltpu.make_async_remote_copy(
            src_ref=src,
            dst_ref=dst,
            send_sem=send,
            recv_sem=recv,
            device_id={"slab": target},
            device_id_type=pl.DeviceIdType.MESH,
        )

    def peer(j):
        return lax.rem(me + j, n)

    barrier = pltpu.get_barrier_semaphore()

    def over_peers(what):
        def one(j, carry):
            what(j)
            return carry

        if n <= 16:
            for j in range(1, n):
                what(j)
        else:
            lax.fori_loop(1, n, one, 0)

    def greet(j):
        pl.semaphore_signal(
            barrier, inc=1, device_id={"slab": peer(j)}, device_id_type=pl.DeviceIdType.MESH
        )

    over_peers(greet)
    for load in loads:
        load.start()

    for a in (raw, a2):
        for side in range(2):

            @pl.when(jnp.logical_not(gets[side]))
            def _():
                a[2 * side] = jnp.zeros(a.shape[1:], BF16)

    pl.semaphore_wait(barrier, n - 1)

    def lat_copy(side, part, half):
        first, end = PAIRS[part]
        cols = pl.ds((first + half * COLS // 2) * 128, (end - first) * 128)
        return remote(
            latent.at[:, cols],
            raw.at[2 * side, :, cols],
            lat_s.at[side],
            lat_r.at[side, part],
            peer(1 if side == 0 else n - 1),
        )

    def arrived(ref, sem):
        remote(ref, ref, sem, sem, me).wait_recv()

    def departed(ref, sem):
        remote(ref, ref, sem, sem, me).wait_send()

    def hid_copy(side, piece):
        first, end = PIECES[piece]
        cols = pl.ds((first + 1) * 128, (end - first) * 128)
        return remote(
            a2.at[1, :, cols],
            a2.at[2 * side, :, cols],
            hid_s.at[side],
            hid_r.at[side, min(piece, 3)],
            peer(1 if side == 0 else n - 1),
        )

    def rim_copy(side, what):
        if what in (2, 5):
            src, dst = edge0.at[side, what // 3], halo0.at[side, what // 3]
        else:
            b, deep = {0: (b1, 0), 1: (b1, 1), 3: (b3, 1), 4: (b1, 2)}[what]
            block = (6 - deep, 3 + deep)[side]
            to = (2 - deep, 7 + deep)[side]
            src, dst = b.at[pl.ds(block * BLOCK, BLOCK)], b.at[pl.ds(to * BLOCK, BLOCK)]
        return remote(
            src,
            dst,
            rim_s.at[side, (0, 0, 0, 1, 2, 2)[what]],
            rim_r.at[side, (0, 1, 1, 2, 3, 3)[what]],
            peer(SHOTS if side == 0 else n - SHOTS),
        )

    rim_sends = (has_high, has_low)
    rim_gets = (has_low, has_high)

    def rows(b):
        return pl.ds(pl.multiple_of(b * BLOCK, BLOCK), BLOCK)

    def own(b):
        return pl.ds(pl.multiple_of((b - OWN) * BLOCK, BLOCK), BLOCK)

    for part in range(len(PAIRS)):
        for side in range(2):

            @pl.when(sends[side])
            def _():
                lat_copy(side, part, 0).start()
                lat_copy(side, part, 1).start()

    loads[1].wait()
    loads[3].wait()
    for w, packed in ((w1, wp1), (w2, wp2)):
        for tap in range(9):
            packed[tap * CH : (tap + 1) * CH] = jnp.concatenate(
                [w[dz * 9 + tap] for dz in range(3)], axis=1
            )

    for side in range(2):
        ext = (2, 7)[side]

        @pl.when(jnp.logical_not(rim_gets[side]))
        def _():
            for f in (f1, f2, f3):
                f[ext * BLOCK : (ext + 1) * BLOCK] = jnp.zeros((BLOCK, FX), F32)

    for f, empty in ((f3, (1, 8)), (f4, (2, 7))):
        for b in empty:
            f[rows(b)] = jnp.zeros((BLOCK, FX), F32)

    for f in (f5, f6):
        f[...] = jnp.zeros(f.shape, F32)

    loads[2].wait()
    loads[12].wait()
    b1[inner] = f1[inner].astype(BF16)
    for side in range(2):
        for deep in range(2):
            edge0[side, deep] = f0[rows((6 - deep, 3 + deep)[side])].astype(BF16)

    middle = (slab == 0) == (shot >= SHOTS // 2)

    def give_rims(at):
        for times, mine in zip(RIMS_AT, (middle, jnp.logical_not(middle))):
            whats = [what for what, t in zip(WHATS, times) if t == at]
            for side in range(2):
                if whats:

                    @pl.when(rim_sends[side] & mine)
                    def _():
                        for what in whats:
                            rim_copy(side, what).start()

    give_rims(-1)
    loads[4].wait()
    loads[15].wait()
    station = receivers[:, shot]
    same = lax.broadcasted_iota(jnp.int32, (128, 128), 0) == lax.broadcasted_iota(
        jnp.int32, (128, 128), 1
    )

    def upright(v):
        return jnp.sum(
            jnp.where(same, jnp.broadcast_to(v.astype(F32), (128, 128)), 0.0), axis=1, keepdims=True
        ).astype(jnp.int32)

    station_row = upright((station[0:1] - slab * FPS) * FY + station[1:2])
    station_col = upright(station[2:3])
    row = lax.broadcasted_iota(jnp.int32, (128, BLOCK), 1)
    for b in range(4):
        hot[b] = (row + b * BLOCK == station_row).astype(F32).astype(BF16)
    at_col = lax.broadcasted_iota(jnp.int32, (128, FX), 1) == station_col
    seen[...] = jnp.zeros(seen.shape, F32)
    rec[...] = jnp.zeros((STEPS, FX), F32)

    square = (CH, CH)
    diagonal = lax.broadcasted_iota(jnp.int32, square, 0) == lax.broadcasted_iota(
        jnp.int32, square, 1
    )
    spread = jnp.broadcast_to(head[...].astype(F32), square)
    head_col[...] = jnp.broadcast_to(
        jnp.sum(jnp.where(diagonal, spread, 0.0), axis=1, keepdims=True), (CH, 128)
    )

    lane = lax.broadcasted_iota(jnp.int32, (1, 128), 1)
    keep_left = lax.rem(lane, CX) > 0
    keep_right = lax.rem(lane, CX) < CX - 1

    def column(a, c):
        return a[:, :, c * 128 : (c + 1) * 128].reshape(3 * CH, 128)

    def put(a, c, v):
        a[:, :, c * 128 : (c + 1) * 128] = v.astype(BF16).reshape(3, CH, 128)

    low_half = lane < CX

    def spread(packed, a, columns):
        block = jnp.concatenate([column(a, j + 1) for j in columns], axis=1)
        got = dot(packed[...], block)
        for i, j in enumerate(columns):
            taps[j] = got[:, i * 128 : (i + 1) * 128].reshape(9, CH, 128)

    def gathered(j):
        sums = []
        for dx in range(3):
            v = taps[j, 3 + dx]
            if j > 0:
                v = v + taps[j - 1, dx]
            else:
                v = v + jnp.where(low_half, 0.0, pltpu.roll(taps[COLS - 1, dx], CX, 1))
            if j < COLS - 1:
                v = v + taps[j + 1, 6 + dx]
            else:
                v = v + jnp.where(low_half, pltpu.roll(taps[0, 6 + dx], CX, 1), 0.0)
            sums.append(v)
        v = (
            sums[1]
            + jnp.where(keep_left, pltpu.roll(sums[0], 1, 1), 0.0)
            + jnp.where(keep_right, pltpu.roll(sums[2], 127, 1), 0.0)
        )
        return jnp.where(v > 0, v, LEAK * v)

    loads[0].wait()
    loads[16].wait()

    def send_hidden(pieces):
        for side in range(2):

            @pl.when(sends[side])
            def _():
                for piece in pieces:
                    hid_copy(side, piece).start()

    for part, (first, end) in enumerate(PAIRS):
        for side in range(2):

            @pl.when(gets[side])
            def _():
                arrived(
                    raw.at[2 * side, :, pl.ds(0, 2 * (end - first) * 128)], lat_r.at[side, part]
                )

        for i in range(first, end):
            pair = jnp.concatenate([column(raw, i), column(raw, i + COLS // 2)], axis=1)
            folded = dot(pair, fold[...])
            put(a1, 2 * i + 1, folded[:, :128])
            put(a1, 2 * i + 2, folded[:, 128:])
        spread(wp1, a1, range(2 * first, 2 * end))
        for j in FIRST[part]:
            a2[1, :, (j + 1) * 128 : (j + 2) * 128] = gathered(j).astype(BF16)
        send_hidden((part, part + 1) if end == COLS // 2 else (part,))
        give_rims(part)

    def beside(now, c, planes):
        return now[pl.ds(pl.multiple_of(c * BLOCK + planes * FY, FY), BLOCK)]

    def in_depth(now, c):
        lap = (SCALE * C[1]) * (beside(now, c, -1) + beside(now, c, 1))
        for k in range(2, 5):
            lap = lap + (SCALE * C[k]) * (beside(now, c, -k) + beside(now, c, k))
        return lap

    def laplace(now, blocks):
        centres = [now[rows(c)] for c in blocks]
        halves = [two(v) for v in centres]
        down = dot(
            along_y[...],
            jnp.concatenate([jnp.concatenate(h, axis=0) for h in halves], axis=1),
        )
        across = dot(
            jnp.concatenate([jnp.concatenate(h, axis=1) for h in halves], axis=0), along_x[...]
        )
        laps = []
        for i, (c, v) in enumerate(zip(blocks, centres)):
            lap = CENTRE * v + down[:, FX * i : FX * (i + 1)]
            lap = lap + across[BLOCK * i : BLOCK * (i + 1)]
            laps.append(lap + in_depth(now, c))
        return laps

    def advance(t, b, lap, v, before):
        pulse = jnp.where(linear == source_at - (b - OWN) * (BLOCK * FX), wavelet[t - 1, shot], 0.0)
        return 2.0 * v - before + pace[rows(b)] * lap + pulse

    def weighted(t, b, lap):
        return adj[t - 1, own(b)].astype(F32) * lap

    def observe(t, b, new):
        hi, lo = two(new)
        got = dot(hot[b - OWN], jnp.concatenate([hi, lo], axis=1))
        seen[t - 1] += got[:, :FX] + got[:, FX:]

    def finish(t, c, lap, now, before, new_f):
        new = advance(t, c, lap, now[rows(c)], before[rows(c)])
        new_f[(own if t == STEPS else rows)(c)] = new
        return new

    def step(t, blocks, now, before, new_f):
        for c, lap in zip(blocks, laplace(now, blocks)):
            finish(t, c, lap, now, before, new_f)
            corr[own(c)] += weighted(t, c, lap)

    for i in (5, 6, 7, 8, 9, 10, 11):
        loads[i].wait()
    source_at = (
        (sources[0, shot] - slab * FPS) * (FY * FX) + sources[1, shot] * FX + sources[2, shot]
    )
    linear = lax.broadcasted_iota(jnp.int32, (BLOCK, FX), 0) * FX + lax.broadcasted_iota(
        jnp.int32, (BLOCK, FX), 1
    )

    def first_laplace(blocks):
        for c, lap in zip(blocks, laplace(f1, blocks)):
            lap1[rows(c)] = lap
            corr[own(c)] = weighted(1, c, lap)

    give_rims(4)
    first_laplace((4, 5))

    def get_hidden(piece):
        for side in range(2):

            @pl.when(gets[side])
            def _():
                arrived(a2.at[2 * side, :, pl.ds(128, 4 * 128)], hid_r.at[side, piece])

    for part, columns in enumerate(SECOND):
        get_hidden(part)
        spread(wp2, a2, FIRST[part])
        for j in columns:
            v = gathered(j) * head_col[...]
            logits[8 * j : 8 * j + 8] = jnp.sum(v.reshape(CH // 8, 8, 128), axis=0)
    give_rims(5)
    total_logits = jnp.sum(logits[...].reshape(COLS, 8, 128), axis=1)
    wave_speed = 1.5 + 3.0 / (1.0 + jnp.exp(-total_logits))
    vel[...] = wave_speed.astype(BF16)

    def vel_copy(k, to_slab, slot, send, recv):
        return remote(vel, vels.at[slot], vel_s.at[send], vel_r.at[recv], to_slab * SHOTS + k)

    lends_low = (shot < REACH) & has_low
    lends_high = (shot >= SHOTS - REACH) & has_high

    def vel_sends():
        @pl.when(lends_low)
        def _():
            for k in range(SHOTS):
                vel_copy(k, slab - 1, lax.rem(shot, REACH) + SHOTS + REACH, 1, 2).start()

        @pl.when(lends_high)
        def _():
            for k in range(SHOTS):
                vel_copy(k, slab + 1, lax.rem(shot + 2, REACH), 2, 1).start()

        for j in range(1, SHOTS):
            vel_copy(lax.rem(shot + j, SHOTS), slab, shot + REACH, 0, 0).start()

    def vel_gets():
        arrived(vels.at[pl.ds(0, SHOTS - 1)], vel_r.at[0])
        for side in range(2):

            @pl.when(rim_gets[side])
            def _():
                arrived(vels.at[pl.ds(0, REACH)], vel_r.at[side + 1])

    def rec_copy(j):
        return remote(rec, recs.at[j], rec_s.at[0], rec_r.at[0], peer(j))

    vel_sends()
    vels[shot + REACH] = vel[...]
    give_rims(6)
    for side in range(2):
        @pl.when(rim_gets[side])
        def _():
            ext = (2, 7)[side]
            arrived(b1.at[pl.ds(0, BLOCK)], rim_r.at[side, 0])
            f1[rows(ext)] = b1[rows(ext)].astype(F32)

    first_laplace((3, 6))
    vel_gets()
    give_rims(7)
    planes = []
    for i in range(3 * GROUP):
        plane = jnp.clip(slab * SHOTS - REACH + i, 0, n - 1)
        planes.append(vels[plane - slab * SHOTS + REACH])
    wide = dot(jnp.concatenate(planes, axis=0), up_x[...])
    tall = []
    for g in range(3):
        part = wide[16 * GROUP * g : 16 * GROUP * (g + 1)]
        hi, lo = two(jnp.concatenate([part[:, :FX], part[:, FX:]], axis=0))
        both = dot(up_y[...], jnp.concatenate([hi, lo], axis=1))
        both = both[:, :FX] + both[:, FX:]
        tall += [both[FY * i : FY * (i + 1)] for i in range(GROUP)]
    def paced(z):
        i = z // 2 + REACH
        fine = 0.75 * doubled[i] + 0.25 * doubled[i + 1 if z % 2 else i - 1]
        at = z * FY + OWN * BLOCK
        if 0 <= z < FPS:
            speed[z * FY : (z + 1) * FY] = fine
        courant = COURANT * fine
        pace[at : at + FY] = courant * courant * (1.0 / SCALE)

    doubled = tall
    for z in range(FPS):
        paced(z)

    n1, n2 = jnp.where(has_low, 3, 6), jnp.where(has_low, 4, 5)
    g1, g2 = 9 - n1, 9 - n2
    far_too = has_low & has_high

    def second(c):
        finish(1, c, lap1[rows(c)], f1, f0, f2)

    for b in (3, 4, 5, 6):
        second(b)
    step(2, (n2,), f2, f1, f3)
    b3[rows(n2)] = f3[rows(n2)].astype(BF16)

    @pl.when(has_low)
    def _():
        rim_copy(1, 3).start()

    @pl.when(has_high & jnp.logical_not(has_low))
    def _():
        rim_copy(0, 3).start()

    step(2, (g2,), f2, f1, f3)

    @pl.when(far_too)
    def _():
        b3[rows(5)] = f3[rows(5)].astype(BF16)
        rim_copy(0, 3).start()

    for z in (*range(-8, 0), *range(FPS, FPS + 8)):
        paced(z)

    def deeper(side):
        ext, far, last = ((2, 1, 0), (7, 8, 9))[side]
        arrived(b1.at[pl.ds(0, 2 * BLOCK)], rim_r.at[side, 1])
        arrived(b1.at[pl.ds(0, 2 * BLOCK)], rim_r.at[side, 3])
        for c in (far, last):
            f1[rows(c)] = b1[rows(c)].astype(F32)
        for i, c in enumerate((ext, far)):
            f0[rows(c)] = halo0[side, i].astype(F32)
        for c, lap in zip((ext, far), laplace(f1, (ext, far))):
            finish(1, c, lap, f1, f0, f2)
        finish(2, ext, laplace(f2, (ext,))[0], f2, f1, f3)

    give_rims(8)
    @pl.when(far_too)
    def _():
        deeper(1)

    step(2, (g1,), f2, f1, f3)
    def collected(first, last):
        parts = []
        for t in range(first, last + 1):
            parts += two(jnp.where(at_col, seen[t - 1], 0.0))
        wide = (8, (last - first + 1) * 2 * FX)
        pick = lax.broadcasted_iota(jnp.int32, wide, 0) == first - 1 + lax.broadcasted_iota(
            jnp.int32, wide, 1
        ) // (2 * FX)
        line = dot(
            pick.astype(F32).astype(BF16), jnp.concatenate(parts, axis=1), ((1,), (1,))
        )
        rec[...] += line[:STEPS]

    for b in (3, 4, 5, 6):
        observe(1, b, f2[rows(b)])
    for b in (g1, g2, n2):
        observe(2, b, f3[rows(b)])
    collected(1, 1)

    @pl.when(far_too)
    def _():
        rim_copy(1, 3).wait_recv()
        f3[rows(8)] = b3[rows(8)].astype(F32)
        finish(3, 7, laplace(f3, (7,))[0], f3, f2, f4)

    step(3, (g1, g2), f3, f2, f4)
    step(4, (g1,), f4, f3, final_out)
    for b in (g1, g2):
        observe(3, b, f4[rows(b)])
    observe(4, g1, final_out[own(g1)])
    loads[13].wait()
    loads[14].wait()

    def raised(c):
        fine = (2.0 * COURANT * COURANT / SCALE) * speed[own(c)] * corr[own(c)]
        return dot(up_zyt[c - OWN], fine.astype(BF16))

    ext, far = jnp.where(has_low, 2, 7), jnp.where(has_low, 1, 8)
    pl.when(has_low)(lambda: deeper(0))
    pl.when(has_high & jnp.logical_not(has_low))(lambda: deeper(1))
    step(2, (n1,), f2, f1, f3)
    step(3, (n2, n1), f3, f2, f4)
    step(4, (g2, n2), f4, f3, final_out)
    lap1[rows(ext)] = laplace(f3, (ext,))[0]
    lap1[rows(n1)] = laplace(f4, (n1,))[0]
    observe(2, n1, f3[rows(n1)])
    for b in (n2, n1):
        observe(3, b, f4[rows(b)])
    for b in (g2, n2):
        observe(4, b, final_out[own(b)])
    collected(2, 3)
    tall = raised(g1) + raised(g2) + raised(n2)
    @pl.when(has_low)
    def _():
        rim_copy(0, 3).wait_recv()

    @pl.when(has_high & jnp.logical_not(has_low))
    def _():
        rim_copy(1, 3).wait_recv()

    f5[rows(far)] = b3[rows(far)].astype(F32)
    lap = lap1[rows(ext)] + in_depth(f5, ext)
    f6[rows(ext)] = advance(3, ext, lap, f3[rows(ext)], f2[rows(ext)])
    lap = lap1[rows(n1)] + in_depth(f6, n1)
    last = finish(4, n1, lap, f4, f3, final_out)
    corr[own(n1)] += weighted(4, n1, lap)
    observe(4, n1, last)
    collected(4, 4)
    tall = tall + raised(n1)
    half = tall.shape[0] // 2
    hi, lo = two(jnp.concatenate([tall[:half], tall[half:]], axis=1))
    narrow = dot(hi, up_xt[...]) + dot(lo, up_xt[...])
    gr[...] = narrow.reshape(SHOTS + 2, 16, FX)
    over_peers(lambda j: rec_copy(j).start())


    @pl.when(jnp.logical_not(has_low))
    def _():
        gr[1] += gr[0]

    @pl.when(jnp.logical_not(has_high))
    def _():
        gr[SHOTS] += gr[SHOTS + 1]

    def gr_copy(j):
        other = lax.rem(shot + j, SHOTS)
        return remote(
            gr.at[other + 1], grs.at[j], gr_s.at[0], gr_r.at[0], slab * SHOTS + other
        )

    def low_copy(slot):
        return remote(
            gr.at[0], grs.at[slot], gr_s.at[1], gr_r.at[1], lax.rem(slab * SHOTS - 1 + n, n)
        )

    def high_copy(slot):
        return remote(
            gr.at[SHOTS + 1],
            grs.at[slot],
            gr_s.at[2],
            gr_r.at[2],
            lax.rem((slab + 1) * SHOTS, n),
        )

    @pl.when(has_low)
    def _():
        low_copy(8 + shot).start()

    @pl.when(has_high)
    def _():
        high_copy(16 + shot).start()

    for j in range(1, SHOTS):
        gr_copy(j).start()


    recs[0] = rec[...]
    arrived(recs.at[pl.ds(1, n - 1)], rec_r.at[0])
    for s in range(SHOTS):

        def slab_term(k, acc):
            return acc + recs[lax.rem(me - (k * SHOTS + s) + n, n)]

        summed = lax.fori_loop(0, slabs, slab_term, jnp.zeros((STEPS, FX), F32))
        traces_out[s] = summed

    arrived(grs.at[pl.ds(1, SHOTS - 1)], gr_r.at[0])
    summed = gr[shot + 1]
    for j in range(1, SHOTS):
        summed = summed + grs[j]
    total[...] = summed

    @pl.when((shot == SHOTS - 1) & has_high)
    def _():
        arrived(grs.at[pl.ds(8, SHOTS)], gr_r.at[1])
        total[...] += jnp.sum(grs[8:16], axis=0)

    @pl.when((shot == 0) & has_low)
    def _():
        arrived(grs.at[pl.ds(16, SHOTS)], gr_r.at[2])
        total[...] += jnp.sum(grs[16:24], axis=0)

    gradient_out[...] = total[...]

    for side in range(2):

        @pl.when(sends[side])
        def _():
            departed(raw.at[0], lat_s.at[side])
            departed(a2.at[1, :, pl.ds(128, CELLS)], hid_s.at[side])

        @pl.when(rim_sends[side])
        def _():
            departed(b1.at[pl.ds(0, 3 * BLOCK)], rim_s.at[side, 0])
            departed(b3.at[pl.ds(0, BLOCK)], rim_s.at[side, 1])
            departed(b1.at[pl.ds(0, 2 * BLOCK)], rim_s.at[side, 2])

    departed(vels.at[pl.ds(0, SHOTS - 1)], vel_s.at[0])

    for lends, sem in ((lends_low, 1), (lends_high, 2)):

        @pl.when(lends)
        def _():
            departed(vels.at[pl.ds(0, SHOTS)], vel_s.at[sem])

    departed(recs.at[pl.ds(1, n - 1)], rec_s.at[0])
    departed(grs.at[pl.ds(1, SHOTS - 1)], gr_s.at[0])

    @pl.when(has_low)
    def _():
        departed(grs.at[0], gr_s.at[1])

    @pl.when(has_high)
    def _():
        departed(grs.at[0], gr_s.at[2])


def hand_over(a, b, c, x, y, z, sem):
    rows = FPS * FY // HALVES
    parts = [
        (a.at[pl.ds(i * rows, rows)], x.at[pl.ds(i * rows, rows)]) for i in range(HALVES)
    ]
    parts += [(b, y), (c, z)]
    copies = [pltpu.make_async_copy(src, dst, sem.at[i]) for i, (src, dst) in enumerate(parts)]
    for copy in copies:
        copy.start()
    for copy in copies:
        copy.wait()


def body(
    n,
    latent,
    conv1_weight,
    conv2_weight,
    head,
    p_prev,
    p_cur,
    adjoint,
    wavelet,
    sources,
    receivers,
):
    along_x, along_y, up_y, up_zyt, up_x, up_xt, fold = constants()
    vmem = pl.BlockSpec(memory_space=pltpu.VMEM)
    hbm = pl.BlockSpec(memory_space=pl.ANY)
    dma = pltpu.SemaphoreType.DMA
    final, traces, gradient = pl.pallas_call(
        functools.partial(kernel, n),
        out_shape=(
            pltpu.VMEM((FPS * FY, FX), F32),
            pltpu.VMEM((SHOTS, STEPS, 128), F32),
            pltpu.VMEM((16, FX), F32),
        ),
        in_specs=[hbm] * 17,
        out_specs=(vmem, vmem, vmem),
        scratch_shapes=[
            pltpu.VMEM((1, CH), BF16),
            pltpu.VMEM(conv1_weight.shape, BF16),
            pltpu.VMEM(conv2_weight.shape, BF16),
            pltpu.SMEM((STEPS, SHOTS), F32),
            pltpu.SMEM((3, SHOTS), jnp.int32),
            pltpu.VMEM((3, SHOTS, 128), jnp.int32),
            pltpu.VMEM(along_x.shape, BF16),
            pltpu.VMEM(along_y.shape, BF16),
            pltpu.VMEM(up_x.shape, BF16),
            pltpu.VMEM(up_xt.shape, BF16),
            pltpu.VMEM((WINDOW, FX), F32),
            pltpu.VMEM((CH, 128), F32),
            pltpu.VMEM((3, CH, CELLS), BF16),
            pltpu.VMEM(fold.shape, BF16),
            pltpu.VMEM((3, CH, (COLS + 2) * 128), BF16),
            pltpu.VMEM((3, CH, (COLS + 2) * 128), BF16),
            pltpu.VMEM((9 * CH, 3 * CH), BF16),
            pltpu.VMEM((9 * CH, 3 * CH), BF16),
            pltpu.VMEM((COLS, 9, CH, 128), F32),
            pltpu.VMEM((COLS * 8, 128), F32),
            pltpu.VMEM((16, FX), BF16),
            pltpu.VMEM((3 * GROUP, 16, FX), BF16),
            *[pltpu.VMEM((WINDOW, FX), F32)] * 7,
            *[pltpu.VMEM((WINDOW, FX), BF16)] * 2,
            pltpu.VMEM((STEPS, FPS * FY, FX), BF16),
            pltpu.VMEM(up_y.shape, BF16),
            pltpu.VMEM(up_zyt.shape, BF16),
            pltpu.VMEM((FPS * FY, FX), F32),
            pltpu.VMEM((FPS * FY, FX), F32),
            pltpu.VMEM((WINDOW, FX), F32),
            pltpu.VMEM((2, 2, BLOCK, FX), BF16),
            pltpu.VMEM((2, 2, BLOCK, FX), BF16),
            pltpu.VMEM((4, 128, BLOCK), BF16),
            pltpu.VMEM((STEPS, 128, FX), F32),
            pltpu.VMEM((STEPS, FX), F32),
            pltpu.VMEM((n, STEPS, FX), F32),
            pltpu.VMEM((SHOTS + 2, 16, FX), F32),
            pltpu.VMEM((3 * SHOTS, 16, FX), F32),
            pltpu.VMEM((16, FX), F32),
            dma((18,)),
            dma((2,)),
            dma((2, 4)),
            dma((2,)),
            dma((2, 4)),
            dma((2, 3)),
            dma((2, 4)),
            dma((3,)),
            dma((3,)),
            dma((1,)),
            dma((1,)),
            dma((3,)),
            dma((3,)),
        ],
        compiler_params=pltpu.CompilerParams(
            collective_id=0, has_side_effects=True, vmem_limit_bytes=VMEM_BYTES
        ),
    )(
        latent.reshape(CH, CELLS),
        conv1_weight,
        conv2_weight,
        head.reshape(1, CH),
        wavelet.T,
        sources.T,
        receivers.transpose(1, 0, 2),
        along_x,
        along_y,
        up_x,
        up_xt,
        p_prev.reshape(FPS * FY, FX),
        p_cur.reshape(FPS * FY, FX),
        adjoint.reshape(STEPS, FPS * FY, FX),
        up_y,
        up_zyt,
        fold,
    )
    final, traces, gradient = pl.pallas_call(
        hand_over,
        out_shape=(
            jax.ShapeDtypeStruct((FPS * FY, FX), F32),
            jax.ShapeDtypeStruct((SHOTS, STEPS, 128), F32),
            jax.ShapeDtypeStruct((16, FX), F32),
        ),
        in_specs=[vmem] * 3,
        out_specs=[hbm] * 3,
        scratch_shapes=[dma((HALVES + 2,))],
    )(*[pltpu.with_memory_space_constraint(v, pltpu.VMEM) for v in (final, traces, gradient)])
    return final.reshape(1, FPS, FY, FX), traces, gradient.reshape(1, CELLS)


def solution(mesh):
    in_specs = (
        P(None, ("groups", "slab"), None),
        P(),
        P(),
        P(),
        P(("groups", "slab"), None, None, None),
        P(("groups", "slab"), None, None, None),
        P(None, ("groups", "slab"), None, None, None),
        P("groups", None),
        P("groups", None),
        P("groups", None, None),
    )
    out_specs = (
        P(("groups", "slab"), None, None, None),
        P("groups", None, None),
        P(("groups", "slab"), None),
    )
    return jax.shard_map(
        functools.partial(body, mesh.shape["slab"]),
        mesh=mesh,
        in_specs=in_specs,
        out_specs=out_specs,
        check_vma=False,
    )
```
